512 devices in a mesh: pair: 32 (over z_hi, y, core), split: 16 (over x, z_lo).
Axes of the slice: x: 4, y: 8, z: 8 (z_hi: 2, z_lo: 4; z = z_hi * 4 + z_lo), core: 2. Of those that a mesh axis runs over, the one named last changes fastest.
Arguments:
- integrals: bfloat16 [8192, 10240], P('pair', 'split'), may hold values from -0.109375 to 0.109375
- normal_ops: bfloat16 [10240, 8192], P('split', 'pair'), may hold values from -6 to 6
- window: int32 [10240], P('split'), may hold values 0 or 1
Outputs:
- complementary: bfloat16 [8192, 8192], P(('pair', 'split'))
The draws below stay inside these ranges and needn't reach their ends.
All inputs are finite; a program needn't handle non-finite values. No bound on the sum of `window` on one device may be relied on, other than what follows from the above.
Results may differ from the reference program's by a relative error of at most 0.001.
Values may be sent and summed in bfloat16 or wider, within the bound.
A program may use at most 64 MiB of HBM per device.

```python
import jax
import jax.numpy as jnp

QS = 640
R = 8192
Q = 10240
BW = 8192
N_SPLIT = 16


def plant(drawn, rng, least, high):
    spot = [jax.random.randint(jax.random.fold_in(rng, axis), (), 0, length) for axis, length in enumerate(drawn.shape)]
    longest = drawn.shape.index(max(drawn.shape))
    beside = spot[:longest] + [(spot[longest] + 1) % drawn.shape[longest]] + spot[longest + 1:]
    return drawn.at[tuple(spot)].set(least).at[tuple(beside)].set(high)


def raised(values, own_key, source, target, blocks, factor):
    def block_of(position):
        return (jnp.arange(values.shape[position]) // (values.shape[position] // blocks)).reshape((-1,) + (1,) * (values.ndim - 1 - position))

    first = jax.random.permutation(own_key, blocks)[block_of(target)]
    other_side = (block_of(target) + blocks // 2) % blocks
    return jnp.where((block_of(source) == first) | (block_of(source) == other_side), factor * values, values)


def shard_levels(rng, shape, pieces, smallest, largest):
    loudness = 1.0
    for dim, blocks in pieces:
        heights = jax.random.uniform(jax.random.fold_in(jax.random.fold_in(rng, 6), dim), (blocks,), jnp.float32, smallest / len(pieces), largest / len(pieces))
        loudness = loudness * jnp.repeat(jnp.exp(heights), shape[dim] // blocks).reshape((-1,) + (1,) * (len(shape) - 1 - dim))
    return loudness


def scatter_about(rng, shape, width, most, cuts=(), kind=jnp.bfloat16):
    factor_of = shard_levels(rng, shape, cuts, -0.22, 0.18) if cuts else 1.0
    drawn = jax.random.normal(rng, shape, jnp.float32) * width * factor_of
    return jnp.minimum(jnp.maximum(drawn, -most), most).astype(kind)


def gaussian_with(rng, shape, deviation, reach, cuts, heavy, kind=jnp.bfloat16):
    values = deviation * jax.random.normal(rng, shape, jnp.float32)
    if cuts:
        values = values * shard_levels(rng, shape, cuts, -0.22, 0.18)
    return jnp.clip(raised(values, jax.random.fold_in(rng, 3), *heavy), -reach, reach).astype(kind)


def setup_inputs(seed: int = 0) -> dict:
    splits = jax.random.split(jax.random.key(seed), 4)
    return {
        "integrals": gaussian_with(splits[0], (R, Q), Q ** -0.5, 0.109375, ((0, 32), (1, 16)), (1, 0, 32, 2.75)),
        "normal_ops": scatter_about(splits[1], (Q, BW), 1.0, 6.0, ((0, 16), (1, 32))),
        "window": plant((jax.random.randint(splits[2], (Q,), 0, 4) < 3).astype(jnp.int32), jax.random.fold_in(splits[2], 1), 0, 1),
    }


def reference(integrals, normal_ops, window):
    windowed = normal_ops * window[:, None].astype(jnp.bfloat16)
    total = jnp.zeros((integrals.shape[0], normal_ops.shape[1]), jnp.float32)
    for index in range(N_SPLIT):
        left = integrals[:, index * QS:(index + 1) * QS]
        right = windowed[index * QS:(index + 1) * QS, :]
        total = total + jnp.dot(left, right, preferred_element_type=jnp.float32)
    return total.astype(jnp.bfloat16)
```

```python
import jax
import jax.numpy as jnp
from jax import lax
from jax.experimental import pallas as pl
from jax.experimental.pallas import tpu as pltpu
from jax.sharding import PartitionSpec as P

MESH = pl.DeviceIdType.MESH
QS = 640
BF16, F32 = jnp.bfloat16, jnp.float32


DELTA = (0, 1, -1, 2, -2, 3, -3, 4)
PLACE = {delta: at for at, delta in enumerate(DELTA)} | {-4: 7}
Z_ORDER = (
    ((0, 1), (0, 2), (0, 3), (0, 4), (1, 1), (1, 2), (1, 3)),
    ((0, 1), (0, 2), (0, 3), (1, 1), (1, 2), (1, 3), (1, 4)),
)
Y_ORDER = tuple(
    tuple((d, j) for d in (1, 2, 3) for j in range(4)) + tuple((4, j) for j in last)
    for last in ((0, 1), (2, 3))
)
BATCHES = (((0, 5), (5, 7), (7, 8)), ((0, 8),))


def schedule():
    events = [(2.5 + 1.8 * j, "a", j) for j in (1, 2, 3)]
    for way in (0, 1):
        events += [(6.0 + 1.64 * (i + 1) + 3.0, "y", (way, i)) for i in range(14)]
        events += [(5.0 + 3.3 * (i + 1) + 2.0, "z", (way, i)) for i in range(7)]
    events.sort(key=lambda event: event[0])
    return [event[1:] for event in events]


def kernel(
    a_ref, b_ref, w_ref, out_ref, am, ab, bb, cb, rb, sb, ob,
    a_s, a_r, y_s, y_r, z_s, z_r, k_s, k_r, x_s, x_r, o_s, o_r,
):
    pair, split = lax.axis_index("pair"), lax.axis_index("split")
    zh, y, core = pair // 16, (pair // 2) % 8, pair % 2
    x, zl = split // 4, split % 4
    z = zh * 4 + zl
    exchange = (zl, zl + 1 - 2 * (zl % 2), (zl + 2) % 4, 3 - zl)

    def device(x=x, y=y, z=z, core=core):
        return (z // 4 * 16 + y * 2 + core, x * 4 + z % 4)

    def remote(src, dst, send, recv, to):
        return pltpu.make_async_remote_copy(
            src_ref=src, dst_ref=dst, send_sem=send, recv_sem=recv, device_id=to, device_id_type=MESH
        )

    def up(v, by, n):
        return (v + by + n) % n

    partners = [device(z=zh * 4 + exchange[j]) for j in (1, 2, 3)]
    partners += [device(y=up(y, d, 8)) for d in range(1, 8)]
    partners += [device(x=up(x, d, 4)) for d in (1, 2, 3)]
    partners += [device(core=1 - core), device(z=up(z, 1, 8)), device(z=up(z, -1, 8))]
    barrier = pltpu.get_barrier_semaphore()
    for partner in partners:
        pl.semaphore_signal(barrier, inc=1, device_id=partner, device_id_type=MESH)

    def k_lanes(z_lo):
        return pl.ds(pl.multiple_of(z_lo * QS, 128), QS)

    def k_rows(z):
        return pl.ds(pl.multiple_of(z * QS, 128), QS)

    my_lanes = pl.ds(pl.multiple_of(core * 128, 128), 128)

    keep = w_ref[...].astype(F32).astype(BF16)
    for xx in range(4):
        for zz in range(4):
            at = (xx * 4 + zz) * 16
            am[zz, xx * 16 : xx * 16 + 16, :] = a_ref[at : at + 16, :] * keep
    ab[0, :, k_lanes(zl)] = am[zl]
    for h in (0, 1):
        bb[h, k_rows(z), my_lanes] = b_ref[:, h * 128 : h * 128 + 128]
    pl.semaphore_wait(barrier, len(partners))

    sent = []

    def start(copy):
        copy.start()
        sent.append(copy)

    def a_copy(j):
        return remote(
            am.at[exchange[j]], ab.at[0, :, k_lanes(zl)], a_s.at[j - 1], a_r.at[j - 1],
            device(z=zh * 4 + exchange[j]),
        )

    def y_copy(way, i):
        d, j = Y_ORDER[way][i]
        sign = (-1, 1)[way]
        lanes = k_lanes(exchange[j])
        return remote(
            ab.at[PLACE[sign * (d - 1)], :, lanes], ab.at[PLACE[sign * d], :, lanes],
            y_s.at[way, i], y_r.at[way, i], device(y=up(y, -sign, 8)),
        )

    def z_copy(way, i):
        h, d = Z_ORDER[way][i]
        sign = (-1, 1)[way]
        piece = bb.at[h, k_rows(up(z, sign * (d - 1), 8)), my_lanes]
        return remote(piece, piece, z_s.at[way, i], z_r.at[way, i], device(z=up(z, -sign, 8)))

    def k_copy(h, away):
        piece = bb.at[h, k_rows(up(z, away, 8)), my_lanes]
        at = (away + 8) % 8
        return remote(piece, piece, k_s.at[h, at], k_r.at[h, at], device(core=1 - core))

    def x_copy(h, batch, d):
        lo, hi = BATCHES[h][batch]
        to = up(x, d, 4)
        at = 3 * h + batch
        return remote(
            cb.at[h, to, lo:hi], rb.at[h, d - 1, lo:hi], x_s.at[at, d - 1], x_r.at[at, d - 1], device(x=to)
        )

    def o_copy(h, place):
        return remote(
            sb.at[h, place], ob.at[h, PLACE[-DELTA[place]]], o_s.at[h, place - 1],
            o_r.at[h, PLACE[-DELTA[place]] - 1], device(y=up(y, DELTA[place], 8)),
        )

    def product(h, lo, hi):
        rows = ab[lo:hi].reshape((hi - lo) * 64, 4 * QS)
        for half in (0, 1):
            part = jnp.dot(
                rows, bb[h, half * 4 * QS : (half + 1) * 4 * QS, :], preferred_element_type=F32
            ).reshape(hi - lo, 4, 16, 256)
            for xx in range(4):
                cb[h, xx, lo:hi, :, half * 256 : half * 256 + 256] = part[:, xx]

    def total(h, batch):
        lo, hi = BATCHES[h][batch]
        for d in (1, 2, 3):
            x_copy(h, batch, d).wait_recv()
        mine = cb[h, x, lo:hi] + rb[h, 0, lo:hi] + rb[h, 1, lo:hi] + rb[h, 2, lo:hi]
        sb[h, lo:hi] = mine.astype(BF16)
        for place in range(max(lo, 1), hi):
            start(o_copy(h, place))

    def place_result(h, place, piece):
        col = up(y, DELTA[place], 8) * 512 + h * 128
        for half in (0, 1):
            for cc in (0, 1):
                to = pl.multiple_of(half * 4096 + col + cc * 256, 128)
                from_ = half * 256 + cc * 128
                out_ref[:, pl.ds(to, 128)] = piece[:, from_ : from_ + 128]

    for j in (1, 2, 3):
        start(a_copy(j))
    for way in (0, 1):
        start(y_copy(way, 0))
        start(z_copy(way, 0))
    start(k_copy(0, 0))
    start(k_copy(1, 0))

    done = set()

    def step(kind, what):
        if kind == "a":
            a_copy(what).wait_recv()
            for way in (0, 1):
                start(y_copy(way, what))
        elif kind == "y":
            way, i = what
            y_copy(way, i).wait_recv()
            d, j = Y_ORDER[way][i]
            if (d + 1, j) in Y_ORDER[way]:
                start(y_copy(way, Y_ORDER[way].index((d + 1, j))))
        else:
            way, i = what
            z_copy(way, i).wait_recv()
            h, d = Z_ORDER[way][i]
            if (h, d + 1) in Z_ORDER[way]:
                start(z_copy(way, Z_ORDER[way].index((h, d + 1))))
            if (h, d) == (0, 2):
                start(z_copy(way, Z_ORDER[way].index((1, 1))))
            start(k_copy(h, (-1, 1)[way] * d))
        done.add((kind, what))

    def wait_cores(h):
        for at in range(8):
            k_copy(h, at).wait_recv()

    h0_done = False
    sums = []
    for kind, what in schedule():
        step(kind, what)
        if not h0_done and all(("z", (way, i)) in done for way in (0, 1) for i in range(7) if Z_ORDER[way][i][0] == 0):
            wait_cores(0)
            h0_done = True
        if h0_done:
            for batch, (lo, hi) in enumerate(BATCHES[0]):
                far = {5: 2, 7: 3, 8: 4}[hi]
                ready = all(
                    ("y", (way, i)) in done for way in (0, 1) for i in range(14) if Y_ORDER[way][i][0] <= far
                )
                if ready and batch not in sums:
                    sums.append(batch)
                    product(0, lo, hi)
                    for d in (2, 1, 3):
                        start(x_copy(0, batch, d))
    wait_cores(1)
    product(1, 0, 8)
    for d in (2, 1, 3):
        start(x_copy(1, 0, d))
    for batch in range(3):
        total(0, batch)
    place_result(0, 0, sb.at[0, 0])
    for place in range(1, 8):
        o_copy(0, PLACE[-DELTA[place]]).wait_recv()
        place_result(0, place, ob.at[0, place])
    total(1, 0)
    place_result(1, 0, sb.at[1, 0])
    for place in range(1, 8):
        o_copy(1, PLACE[-DELTA[place]]).wait_recv()
        place_result(1, place, ob.at[1, place])
    for copy in sent:
        copy.wait_send()


def on_device(integrals, normal_ops, window):
    dma = pltpu.SemaphoreType.DMA
    vmem = pl.BlockSpec(memory_space=pltpu.VMEM)
    return pl.pallas_call(
        kernel,
        out_shape=jax.ShapeDtypeStruct((16, 8192), BF16),
        in_specs=[vmem] * 3,
        out_specs=vmem,
        scratch_shapes=[
            pltpu.VMEM((4, 64, QS), BF16),
            pltpu.VMEM((8, 64, 4 * QS), BF16),
            pltpu.VMEM((2, 8 * QS, 256), BF16),
            pltpu.VMEM((2, 4, 8, 16, 512), F32),
            pltpu.VMEM((2, 3, 8, 16, 512), F32),
            pltpu.VMEM((2, 8, 16, 512), BF16),
            pltpu.VMEM((2, 8, 16, 512), BF16),
            dma((3,)), dma((3,)),
            dma((2, 14)), dma((2, 14)),
            dma((2, 7)), dma((2, 7)),
            dma((2, 8)), dma((2, 8)),
            dma((4, 3)), dma((4, 3)),
            dma((2, 7)), dma((2, 7)),
        ],
        compiler_params=pltpu.CompilerParams(
            collective_id=0, has_side_effects=True, vmem_limit_bytes=48 << 20
        ),
        cost_estimate=pl.CostEstimate(flops=2 * 512 * 1024 * 2560, bytes_accessed=1 << 20, transcendentals=0),
    )(integrals, normal_ops, window.reshape(1, QS))


def solution(mesh):
    placed = (P("pair", "split"), P("split", "pair"), P("split"))
    return jax.shard_map(
        on_device, mesh=mesh, in_specs=placed, out_specs=P(("pair", "split"), None), check_vma=False
    )
```

```python
import jax
import jax.numpy as jnp
from jax import lax
from jax.experimental import pallas as pl
from jax.experimental.pallas import tpu as pltpu
from jax.sharding import PartitionSpec as P

MESH = pl.DeviceIdType.MESH
QS = 640
BF16, F32 = jnp.bfloat16, jnp.float32


DELTA = (0, 1, -1, 2, -2, 3, -3, 4)
PLACE = {delta: at for at, delta in enumerate(DELTA)} | {-4: 7}
Z_ORDER = tuple(
    tuple((h, d, k) for h in (0, 1) for d in (1, 2, 3, 4) for k in (0, 1) if d < 4 or k == way) for way in (0, 1)
)
KS = QS // 2
Y_ORDER = tuple(
    tuple((d, j) for d in (1, 2, 3) for j in range(4)) + tuple((4, j) for j in last)
    for last in ((0, 1), (2, 3))
)
BATCHES = (((0, 5), (5, 7), (7, 8)), ((0, 8),))


def schedule(latency=2.2, piece=1.64):
    free, coming, order = {}, [], []

    def send(axis, way, what, load=1.0):
        end = max(send.now, free.get((axis, way), 0.0)) + load * piece
        free[axis, way] = end
        coming.append((end + latency, len(order) + len(coming), axis, way, what))

    send.now = 0.0
    for way in (0, 1):
        send("y", way, 0)
        for j, k in ((1, 0), (2, 1), (3, None)):
            send("z", way, ("a", j), 1.0 if j == 1 else 1.5)
            if k is not None:
                send("z", way, Z_ORDER[way].index((0, 1, k)))
    while coming:
        coming.sort()
        send.now, _, axis, way, what = coming.pop(0)
        if isinstance(what, tuple):
            if way == 0:
                order.append(what)
                for to in (0, 1):
                    send("y", to, what[1])
            continue
        order.append((axis, (way, what)))
        for after in follow_y(way, what) if axis == "y" else follow_z(way, what):
            send(axis, way, after)
    return order


def follow_y(way, i):
    d, j = Y_ORDER[way][i]
    return [Y_ORDER[way].index((d + 1, j))] if (d + 1, j) in Y_ORDER[way] else []


def follow_z(way, i):
    h, d, k = Z_ORDER[way][i]
    after = [(h, d + 1, k)] if (h, d + 1, k) in Z_ORDER[way] else []
    after += {(0, 1, 1): [(1, 1, 0)], (0, 2, 1): [(1, 1, 1)]}.get((h, d, k), [])
    return [Z_ORDER[way].index(piece) for piece in after]


def kernel(
    a_ref, b_ref, w_ref, out_ref, av, wv, am, ab, bb, cb, rb, sb, ob,
    l_s, a_s, a_r, y_s, y_r, z_s, z_r, k_s, k_r, x_s, x_r, o_s, o_r,
):
    pair, split = lax.axis_index("pair"), lax.axis_index("split")
    zh, y, core = pair // 16, (pair // 2) % 8, pair % 2
    x, zl = split // 4, split % 4
    z = zh * 4 + zl
    exchange = (zl, zl + 1 - 2 * (zl % 2), (zl + 2) % 4, 3 - zl)

    def device(x=x, y=y, z=z, core=core):
        return (z // 4 * 16 + y * 2 + core, x * 4 + z % 4)

    def remote(src, dst, send, recv, to):
        return pltpu.make_async_remote_copy(
            src_ref=src, dst_ref=dst, send_sem=send, recv_sem=recv, device_id=to, device_id_type=MESH
        )

    def up(v, by, n):
        return (v + by + n) % n

    partners = [device(z=zh * 4 + exchange[j]) for j in (1, 2, 3)]
    partners += [device(y=up(y, d, 8)) for d in range(1, 8)]
    partners += [device(x=up(x, d, 4)) for d in (1, 2, 3)]
    partners += [device(core=1 - core), device(z=up(z, 1, 8)), device(z=up(z, -1, 8))]
    barrier = pltpu.get_barrier_semaphore()
    for partner in partners:
        pl.semaphore_signal(barrier, inc=1, device_id=partner, device_id_type=MESH)

    def k_lanes(z_lo):
        return pl.ds(pl.multiple_of(z_lo * QS, 128), QS)

    def k_rows(z, k=None):
        if k is None:
            return pl.ds(pl.multiple_of(z * QS, 64), QS)
        return pl.ds(pl.multiple_of(z * QS + k * KS, 64), KS)

    my_lanes = pl.ds(pl.multiple_of(core * 128, 128), 128)

    loads = [
        pltpu.make_async_copy(w_ref, wv, l_s.at[0]),
        pltpu.make_async_copy(a_ref, av, l_s.at[1]),
    ] + [
        pltpu.make_async_copy(b_ref.at[:, pl.ds(h * 128, 128)], bb.at[h, k_rows(z), my_lanes], l_s.at[2 + h])
        for h in (0, 1)
    ]
    for load in loads:
        load.start()
    cb[1] = jnp.zeros(cb.shape[1:], F32)
    for load in loads[:2]:
        load.wait()
    keep = wv[...].astype(F32).astype(BF16).reshape(1, QS)
    for xx in range(4):
        for zz in range(4):
            at = (xx * 4 + zz) * 16
            am[zz, xx * 16 : xx * 16 + 16, :] = av[at : at + 16, :] * keep
    ab[0, :, k_lanes(zl)] = am[zl]
    for load in loads[2:]:
        load.wait()
    pl.semaphore_wait(barrier, len(partners))

    sent = []

    def start(copy):
        copy.start()
        sent.append(copy)

    def a_copy(j):
        return remote(
            am.at[exchange[j]], ab.at[0, :, k_lanes(zl)], a_s.at[j - 1], a_r.at[j - 1],
            device(z=zh * 4 + exchange[j]),
        )

    def y_copy(way, i):
        d, j = Y_ORDER[way][i]
        sign = (-1, 1)[way]
        lanes = k_lanes(exchange[j])
        return remote(
            ab.at[PLACE[sign * (d - 1)], :, lanes], ab.at[PLACE[sign * d], :, lanes],
            y_s.at[way, i], y_r.at[way, i], device(y=up(y, -sign, 8)),
        )

    def z_copy(way, i):
        h, d, k = Z_ORDER[way][i]
        sign = (-1, 1)[way]
        piece = bb.at[h, k_rows(up(z, sign * (d - 1), 8), k), my_lanes]
        return remote(piece, piece, z_s.at[way, i], z_r.at[way, i], device(z=up(z, -sign, 8)))

    def k_copy(h, away, k):
        piece = bb.at[h, k_rows(up(z, away, 8), k), my_lanes]
        at = (away + 8) % 8 * 2 + k
        return remote(piece, piece, k_s.at[h, at], k_r.at[h, at], device(core=1 - core))

    def x_copy(h, batch, d):
        lo, hi = BATCHES[h][batch]
        to = up(x, d, 4)
        at = 3 * h + batch
        return remote(
            cb.at[h, to, lo:hi], rb.at[h, d - 1, lo:hi], x_s.at[at, d - 1], x_r.at[at, d - 1], device(x=to)
        )

    def o_copy(h, place):
        return remote(
            sb.at[h, place], ob.at[h, PLACE[-DELTA[place]]], o_s.at[h, place - 1],
            o_r.at[h, PLACE[-DELTA[place]] - 1], device(y=up(y, DELTA[place], 8)),
        )

    def product(h, lo, hi):
        rows = ab[lo:hi].reshape((hi - lo) * 64, 4 * QS)
        for half in (0, 1):
            part = jnp.dot(
                rows, bb[h, half * 4 * QS : (half + 1) * 4 * QS, :], preferred_element_type=F32
            ).reshape(hi - lo, 4, 16, 256)
            for xx in range(4):
                cb[h, xx, lo:hi, :, half * 256 : half * 256 + 256] = part[:, xx]

    def total(h, batch):
        lo, hi = BATCHES[h][batch]
        for d in (1, 2, 3):
            x_copy(h, batch, d).wait_recv()
        mine = cb[h, x, lo:hi] + rb[h, 0, lo:hi] + rb[h, 1, lo:hi] + rb[h, 2, lo:hi]
        sb[h, lo:hi] = mine.astype(BF16)
        for place in range(max(lo, 1), hi):
            start(o_copy(h, place))

    def place_result(h, place, piece):
        col = up(y, DELTA[place], 8) * 512 + h * 128
        for half in (0, 1):
            for cc in (0, 1):
                to = pl.multiple_of(half * 4096 + col + cc * 256, 128)
                from_ = half * 256 + cc * 128
                out_ref[:, pl.ds(to, 128)] = piece[:, from_ : from_ + 128]

    for way in (0, 1):
        start(y_copy(way, 0))
    for j, k in ((1, 0), (2, 1), (3, None)):
        start(a_copy(j))
        if k is not None:
            for way in (0, 1):
                start(z_copy(way, Z_ORDER[way].index((0, 1, k))))
    for h in (0, 1):
        for k in (0, 1):
            start(k_copy(h, 0, k))

    done = set()

    def step(kind, what):
        if kind == "a":
            a_copy(what).wait_recv()
            for way in (0, 1):
                start(y_copy(way, what))
        elif kind == "y":
            way, i = what
            y_copy(way, i).wait_recv()
            for after in follow_y(way, i):
                start(y_copy(way, after))
        else:
            way, i = what
            z_copy(way, i).wait_recv()
            for after in follow_z(way, i):
                start(z_copy(way, after))
            h, d, k = Z_ORDER[way][i]
            start(k_copy(h, (-1, 1)[way] * d, k))
        done.add((kind, what))

    def wait_core(h, at):
        for k in (0, 1):
            k_copy(h, at, k).wait_recv()

    def add_product(at):
        owner = up(z, at, 8)
        lanes = pl.ds(pl.multiple_of(owner // 4 * 256, 128), 256)
        part = jnp.dot(
            ab[:, :, k_lanes(owner % 4)].reshape(512, QS), bb[1, k_rows(owner), :], preferred_element_type=F32
        ).reshape(8, 4, 16, 256)
        for xx in range(4):
            cb[1, xx, :, :, lanes] += part[:, xx]

    h0_done = False
    sums = []
    for kind, what in schedule():
        step(kind, what)
        if not h0_done and all(("z", (way, i)) in done for way in (0, 1) for i in range(14) if Z_ORDER[way][i][0] == 0):
            for at in range(8):
                wait_core(0, at)
            h0_done = True
        if h0_done:
            for batch, (lo, hi) in enumerate(BATCHES[0]):
                far = {5: 2, 7: 3, 8: 4}[hi]
                ready = all(
                    ("y", (way, i)) in done for way in (0, 1) for i in range(14) if Y_ORDER[way][i][0] <= far
                )
                if ready and batch not in sums:
                    sums.append(batch)
                    product(0, lo, hi)
                    for d in (2, 1, 3):
                        start(x_copy(0, batch, d))
    for at in (0, 1, 7, 2, 6, 3, 5, 4):
        wait_core(1, at)
        add_product(at)
    for d in (2, 1, 3):
        start(x_copy(1, 0, d))
    for batch in range(3):
        total(0, batch)
    place_result(0, 0, sb.at[0, 0])
    for place in range(1, 8):
        o_copy(0, PLACE[-DELTA[place]]).wait_recv()
        place_result(0, place, ob.at[0, place])
    total(1, 0)
    place_result(1, 0, sb.at[1, 0])
    for place in range(1, 8):
        o_copy(1, PLACE[-DELTA[place]]).wait_recv()
        place_result(1, place, ob.at[1, place])
    for copy in sent:
        copy.wait_send()


def on_device(integrals, normal_ops, window):
    dma = pltpu.SemaphoreType.DMA
    vmem = pl.BlockSpec(memory_space=pltpu.VMEM)
    return pl.pallas_call(
        kernel,
        out_shape=jax.ShapeDtypeStruct((16, 8192), BF16),
        in_specs=[pl.BlockSpec(memory_space=pl.ANY)] * 3,
        out_specs=vmem,
        scratch_shapes=[
            pltpu.VMEM((256, QS), BF16),
            pltpu.VMEM((QS,), jnp.int32),
            pltpu.VMEM((4, 64, QS), BF16),
            pltpu.VMEM((8, 64, 4 * QS), BF16),
            pltpu.VMEM((2, 8 * QS, 256), BF16),
            pltpu.VMEM((2, 4, 8, 16, 512), F32),
            pltpu.VMEM((2, 3, 8, 16, 512), F32),
            pltpu.VMEM((2, 8, 16, 512), BF16),
            pltpu.VMEM((2, 8, 16, 512), BF16),
            dma((4,)),
            dma((3,)), dma((3,)),
            dma((2, 14)), dma((2, 14)),
            dma((2, 14)), dma((2, 14)),
            dma((2, 16)), dma((2, 16)),
            dma((4, 3)), dma((4, 3)),
            dma((2, 7)), dma((2, 7)),
        ],
        compiler_params=pltpu.CompilerParams(
            collective_id=0, has_side_effects=True, vmem_limit_bytes=54848 << 10
        ),
        cost_estimate=pl.CostEstimate(flops=2 * 512 * 1024 * 2560, bytes_accessed=1 << 20, transcendentals=0),
    )(integrals, normal_ops, window)


def solution(mesh):
    placed = (P("pair", "split"), P("split", "pair"), P("split"))
    return jax.shard_map(
        on_device, mesh=mesh, in_specs=placed, out_specs=P(("pair", "split"), None), check_vma=False
    )
```

```python
import jax
import jax.numpy as jnp
from jax import lax
from jax.experimental import pallas as pl
from jax.experimental.pallas import tpu as pltpu
from jax.sharding import PartitionSpec as P

MESH = pl.DeviceIdType.MESH
QS = 640
BF16, F32 = jnp.bfloat16, jnp.float32


DELTA = (0, 1, -1, 2, -2, 3, -3, 4)
PLACE = {delta: at for at, delta in enumerate(DELTA)} | {-4: 7}
Z_ORDER = tuple(
    tuple((h, d, k) for h in (0, 1) for d in (1, 2, 3, 4) for k in range(4) if d < 4 or k // 2 == way) for way in (0, 1)
)
KS = QS // 4
Y_ORDER = tuple(
    tuple((d, j) for d in (1, 2, 3) for j in range(4)) + tuple((4, j) for j in last)
    for last in ((0, 1), (2, 3))
)
BATCHES = (((0, 5), (5, 7), (7, 8)), ((4, 8), (0, 4)))
MOST = 32767.0
FIRST = ((1, (0, 1)), (2, (2, 3)), (3, ()))


def schedule(latency=2.2, piece=1.64):
    free, coming, order = {}, [], []

    def send(axis, way, what, load=1.0):
        end = max(send.now, free.get((axis, way), 0.0)) + load * piece
        free[axis, way] = end
        coming.append((end + latency, len(order) + len(coming), axis, way, what))

    send.now = 0.0
    for way in (0, 1):
        send("y", way, 0)
        for j, runs in FIRST:
            send("z", way, ("a", j), 1.0 if j == 1 else 1.5)
            for k in runs:
                send("z", way, Z_ORDER[way].index((0, 1, k)), 0.5)
    while coming:
        coming.sort()
        send.now, _, axis, way, what = coming.pop(0)
        if isinstance(what, tuple):
            if way == 0:
                order.append(what)
                for to in (0, 1):
                    send("y", to, what[1])
            continue
        order.append((axis, (way, what)))
        for after in follow_y(way, what) if axis == "y" else follow_z(way, what):
            send(axis, way, after, 1.0 if axis == "y" else 0.5)
    return order


def follow_y(way, i):
    d, j = Y_ORDER[way][i]
    return [Y_ORDER[way].index((d + 1, j))] if (d + 1, j) in Y_ORDER[way] else []


def follow_z(way, i):
    h, d, k = Z_ORDER[way][i]
    after = [(h, d + 1, k)] if (h, d + 1, k) in Z_ORDER[way] else []
    if (h, d) == (0, 3):
        after.append((1, 1, k))
    return [Z_ORDER[way].index(piece) for piece in after]


def kernel(
    a_ref, b_ref, w_ref, out_ref, av, wv, am, ab, bb, cb, qb, qs, rb, rs, sb, ob,
    l_s, a_s, a_r, y_s, y_r, z_s, z_r, k_s, k_r, x_s, x_r, o_s, o_r,
):
    pair, split = lax.axis_index("pair"), lax.axis_index("split")
    zh, y, core = pair // 16, (pair // 2) % 8, pair % 2
    x, zl = split // 4, split % 4
    z = zh * 4 + zl
    exchange = (zl, zl + 1 - 2 * (zl % 2), (zl + 2) % 4, 3 - zl)

    def device(x=x, y=y, z=z, core=core):
        return (z // 4 * 16 + y * 2 + core, x * 4 + z % 4)

    def remote(src, dst, send, recv, to):
        return pltpu.make_async_remote_copy(
            src_ref=src, dst_ref=dst, send_sem=send, recv_sem=recv, device_id=to, device_id_type=MESH
        )

    def up(v, by, n):
        return (v + by + n) % n

    partners = [device(z=zh * 4 + exchange[j]) for j in (1, 2, 3)]
    partners += [device(y=up(y, d, 8)) for d in range(1, 8)]
    partners += [device(x=up(x, d, 4)) for d in (1, 2, 3)]
    partners += [device(core=1 - core), device(z=up(z, 1, 8)), device(z=up(z, -1, 8))]
    barrier = pltpu.get_barrier_semaphore()
    for partner in partners:
        pl.semaphore_signal(barrier, inc=1, device_id=partner, device_id_type=MESH)

    def k_lanes(z_lo):
        return pl.ds(pl.multiple_of(z_lo * QS, 128), QS)

    def k_rows(z, k=None):
        if k is None:
            return pl.ds(pl.multiple_of(z * QS, 64), QS)
        return pl.ds(pl.multiple_of(z * QS + k * KS, 32), KS)

    my_lanes = pl.ds(pl.multiple_of(core * 128, 128), 128)

    loads = [
        pltpu.make_async_copy(w_ref, wv, l_s.at[0]),
        pltpu.make_async_copy(a_ref, av, l_s.at[1]),
    ] + [
        pltpu.make_async_copy(b_ref.at[:, pl.ds(h * 128, 128)], bb.at[h, k_rows(z), my_lanes], l_s.at[2 + h])
        for h in (0, 1)
    ]
    for load in loads:
        load.start()
    cb[1] = jnp.zeros(cb.shape[1:], F32)
    qs[...] = jnp.zeros(qs.shape, F32)
    for load in loads[:2]:
        load.wait()
    keep = wv[...].astype(F32).astype(BF16).reshape(1, QS)
    for xx in range(4):
        for zz in range(4):
            at = (xx * 4 + zz) * 16
            am[zz, xx * 16 : xx * 16 + 16, :] = av[at : at + 16, :] * keep
    ab[0, :, k_lanes(zl)] = am[zl]
    for load in loads[2:]:
        load.wait()
    pl.semaphore_wait(barrier, len(partners))

    sent = []

    def start(copy):
        copy.start()
        sent.append(copy)

    def a_copy(j):
        return remote(
            am.at[exchange[j]], ab.at[0, :, k_lanes(zl)], a_s.at[j - 1], a_r.at[j - 1],
            device(z=zh * 4 + exchange[j]),
        )

    def y_copy(way, i):
        d, j = Y_ORDER[way][i]
        sign = (-1, 1)[way]
        lanes = k_lanes(exchange[j])
        return remote(
            ab.at[PLACE[sign * (d - 1)], :, lanes], ab.at[PLACE[sign * d], :, lanes],
            y_s.at[way, i], y_r.at[way, i], device(y=up(y, -sign, 8)),
        )

    def z_copy(way, i):
        h, d, k = Z_ORDER[way][i]
        sign = (-1, 1)[way]
        piece = bb.at[h, k_rows(up(z, sign * (d - 1), 8), k), my_lanes]
        return remote(piece, piece, z_s.at[way, i], z_r.at[way, i], device(z=up(z, -sign, 8)))

    def k_copy(h, away, k):
        rows = pl.ds(pl.multiple_of(up(z, away, 8) * QS + k * 2 * KS, 64), 2 * KS)
        piece = bb.at[h, rows, my_lanes]
        at = (away + 8) % 8 * 2 + k
        return remote(piece, piece, k_s.at[h, at], k_r.at[h, at], device(core=1 - core))

    def x_copies(h, batch, d):
        lo, hi = BATCHES[h][batch]
        at = 3 * h + batch
        return (
            remote(
                qb.at[h, d - 1, lo:hi], rb.at[h, d - 1, lo:hi], x_s.at[at, d - 1, 0], x_r.at[at, d - 1, 0],
                device(x=up(x, d, 4)),
            ),
            remote(
                qs.at[at, d - 1], rs.at[at, d - 1], x_s.at[at, d - 1, 1], x_r.at[at, d - 1, 1],
                device(x=up(x, d, 4)),
            ),
        )

    def send_sums(h, batch):
        lo, hi = BATCHES[h][batch]
        at = 3 * h + batch
        for d in (2, 1, 3):
            part = cb[h, up(x, d, 4), lo:hi]
            top = jnp.maximum(jnp.max(jnp.abs(part), axis=1, keepdims=True), 1e-30)
            qb[h, d - 1, lo:hi] = jnp.round(part * (MOST / top)).astype(jnp.int32).astype(jnp.int16)
            qs[at, d - 1, 0 : hi - lo, :] = (top * (1.0 / MOST)).reshape(hi - lo, 512)
            for copy in x_copies(h, batch, d):
                start(copy)

    def o_copy(h, place):
        return remote(
            sb.at[h, place], ob.at[h, PLACE[-DELTA[place]]], o_s.at[h, place - 1],
            o_r.at[h, PLACE[-DELTA[place]] - 1], device(y=up(y, DELTA[place], 8)),
        )

    def product(h, lo, hi):
        rows = ab[lo:hi].reshape((hi - lo) * 64, 4 * QS)
        for half in (0, 1):
            part = jnp.dot(
                rows, bb[h, half * 4 * QS : (half + 1) * 4 * QS, :], preferred_element_type=F32
            ).reshape(hi - lo, 4, 16, 256)
            for xx in range(4):
                cb[h, xx, lo:hi, :, half * 256 : half * 256 + 256] = part[:, xx]

    def total(h, batch):
        lo, hi = BATCHES[h][batch]
        at = 3 * h + batch
        mine = cb[h, x, lo:hi]
        for d in (1, 2, 3):
            for copy in x_copies(h, batch, d):
                copy.wait_recv()
            step = rs[at, d - 1, 0 : hi - lo, :].reshape(hi - lo, 1, 512)
            mine += rb[h, d - 1, lo:hi].astype(jnp.int32).astype(F32) * step
        sb[h, lo:hi] = mine.astype(BF16)
        for place in range(max(lo, 1), hi):
            start(o_copy(h, place))

    def place_result(h, place, piece):
        col = up(y, DELTA[place], 8) * 512 + h * 128
        for half in (0, 1):
            for cc in (0, 1):
                to = pl.multiple_of(half * 4096 + col + cc * 256, 128)
                from_ = half * 256 + cc * 128
                out_ref[:, pl.ds(to, 128)] = piece[:, from_ : from_ + 128]

    for way in (0, 1):
        start(y_copy(way, 0))
    for j, runs in FIRST:
        start(a_copy(j))
        for k in runs:
            for way in (0, 1):
                start(z_copy(way, Z_ORDER[way].index((0, 1, k))))
    for h in (0, 1):
        for k in (0, 1):
            start(k_copy(h, 0, k))

    done = set()

    def step(kind, what):
        if kind == "a":
            a_copy(what).wait_recv()
            for way in (0, 1):
                start(y_copy(way, what))
        elif kind == "y":
            way, i = what
            y_copy(way, i).wait_recv()
            for after in follow_y(way, i):
                start(y_copy(way, after))
        else:
            way, i = what
            z_copy(way, i).wait_recv()
            for after in follow_z(way, i):
                start(z_copy(way, after))
            h, d, k = Z_ORDER[way][i]
            if k % 2:
                start(k_copy(h, (-1, 1)[way] * d, k // 2))
        done.add((kind, what))

    def wait_core(h, at):
        for k in (0, 1):
            k_copy(h, at, k).wait_recv()

    def add_product(at):
        owner = up(z, at, 8)
        lanes = pl.ds(pl.multiple_of(owner // 4 * 256, 128), 256)
        part = jnp.dot(
            ab[:, :, k_lanes(owner % 4)].reshape(512, QS), bb[1, k_rows(owner), :], preferred_element_type=F32
        ).reshape(8, 4, 16, 256)
        for xx in range(4):
            cb[1, xx, :, :, lanes] += part[:, xx]

    h0_done = False
    sums = []
    for kind, what in schedule():
        step(kind, what)
        if not h0_done and all(("z", (way, i)) in done for way in (0, 1) for i in range(28) if Z_ORDER[way][i][0] == 0):
            for at in range(8):
                wait_core(0, at)
            h0_done = True
        if h0_done:
            for batch, (lo, hi) in enumerate(BATCHES[0]):
                far = {5: 2, 7: 3, 8: 4}[hi]
                ready = all(
                    ("y", (way, i)) in done for way in (0, 1) for i in range(14) if Y_ORDER[way][i][0] <= far
                )
                if ready and batch not in sums:
                    sums.append(batch)
                    product(0, lo, hi)
                    send_sums(0, batch)
    for at in (0, 1, 7, 2, 6, 3, 5, 4):
        wait_core(1, at)
        add_product(at)
    for batch in (0, 1):
        send_sums(1, batch)
    for batch in range(3):
        total(0, batch)
    place_result(0, 0, sb.at[0, 0])
    for place in range(1, 8):
        o_copy(0, PLACE[-DELTA[place]]).wait_recv()
        place_result(0, place, ob.at[0, place])
    total(1, 0)
    total(1, 1)
    place_result(1, 0, sb.at[1, 0])
    for place in range(1, 8):
        o_copy(1, PLACE[-DELTA[place]]).wait_recv()
        place_result(1, place, ob.at[1, place])
    for copy in sent:
        copy.wait_send()


def on_device(integrals, normal_ops, window):
    dma = pltpu.SemaphoreType.DMA
    vmem = pl.BlockSpec(memory_space=pltpu.VMEM)
    return pl.pallas_call(
        kernel,
        out_shape=jax.ShapeDtypeStruct((16, 8192), BF16),
        in_specs=[pl.BlockSpec(memory_space=pl.ANY)] * 3,
        out_specs=vmem,
        scratch_shapes=[
            pltpu.VMEM((256, QS), BF16),
            pltpu.VMEM((QS,), jnp.int32),
            pltpu.VMEM((4, 64, QS), BF16),
            pltpu.VMEM((8, 64, 4 * QS), BF16),
            pltpu.VMEM((2, 8 * QS, 256), BF16),
            pltpu.VMEM((2, 4, 8, 16, 512), F32),
            pltpu.VMEM((2, 3, 8, 16, 512), jnp.int16),
            pltpu.VMEM((5, 3, 8, 512), F32),
            pltpu.VMEM((2, 3, 8, 16, 512), jnp.int16),
            pltpu.VMEM((5, 3, 8, 512), F32),
            pltpu.VMEM((2, 8, 16, 512), BF16),
            pltpu.VMEM((2, 8, 16, 512), BF16),
            dma((4,)),
            dma((3,)), dma((3,)),
            dma((2, 14)), dma((2, 14)),
            dma((2, 28)), dma((2, 28)),
            dma((2, 16)), dma((2, 16)),
            dma((5, 3, 2)), dma((5, 3, 2)),
            dma((2, 7)), dma((2, 7)),
        ],
        compiler_params=pltpu.CompilerParams(
            collective_id=0, has_side_effects=True, vmem_limit_bytes=54848 << 10
        ),
        cost_estimate=pl.CostEstimate(flops=2 * 512 * 1024 * 2560, bytes_accessed=1 << 20, transcendentals=0),
    )(integrals, normal_ops, window)


def solution(mesh):
    placed = (P("pair", "split"), P("split", "pair"), P("split"))
    return jax.shard_map(
        on_device, mesh=mesh, in_specs=placed, out_specs=P(("pair", "split"), None), check_vma=False
    )
```

```python
import jax
import jax.numpy as jnp
from jax import lax
from jax.experimental import pallas as pl
from jax.experimental.pallas import tpu as pltpu
from jax.sharding import PartitionSpec as P

MESH = pl.DeviceIdType.MESH
QS = 640
BF16, F32 = jnp.bfloat16, jnp.float32


DELTA = (0, 1, -1, 2, -2, 3, -3, 4)
PLACE = {delta: at for at, delta in enumerate(DELTA)} | {-4: 7}
Z_ORDER = tuple(
    tuple((h, d, k) for h in (0, 1) for d in (1, 2, 3, 4) for k in range(4) if d < 4 or k // 2 == way) for way in (0, 1)
)
KS = QS // 4
Y_ORDER = tuple(
    tuple((d, j) for d in (1, 2, 3) for j in range(4)) + tuple((4, j) for j in last)
    for last in ((0, 1), (2, 3))
)
BATCHES = (((0, 4), (4, 8)), ((4, 8), (0, 4)))
MOST = 32767.0
NEAR_FIRST = (0, 1, 7, 2, 6, 3, 5, 4)
FIRST = (("a", 1), ("z", (0, 1)), ("a", 2), ("z", (2, 3)), ("a", 3))


def schedule(latency=3.2, piece=1.64):
    free, coming, order = {}, [], []

    def send(axis, way, what, load=1.0):
        end = max(send.now, free.get((axis, way), 0.0)) + load * piece
        free[axis, way] = end
        coming.append((end + latency, len(order) + len(coming), axis, way, what))

    send.now = 0.0
    for way in (0, 1):
        send("y", way, 0)
        for kind, what in FIRST:
            if kind == "a":
                send("z", way, ("a", what), 1.0 if what == 1 else 1.5)
            else:
                for k in what:
                    send("z", way, Z_ORDER[way].index((0, 1, k)), 0.5)
    while coming:
        coming.sort()
        send.now, _, axis, way, what = coming.pop(0)
        if isinstance(what, tuple):
            if way == 0:
                order.append(what)
                for to in (0, 1):
                    send("y", to, what[1])
            continue
        order.append((axis, (way, what)))
        for after in follow_y(way, what) if axis == "y" else follow_z(way, what):
            send(axis, way, after, 1.0 if axis == "y" else 0.5)
    return order


def follow_y(way, i):
    d, j = Y_ORDER[way][i]
    return [Y_ORDER[way].index((d + 1, j))] if (d + 1, j) in Y_ORDER[way] else []


def follow_z(way, i):
    h, d, k = Z_ORDER[way][i]
    after = [(h, d + 1, k)] if (h, d + 1, k) in Z_ORDER[way] else []
    if (h, d) == (0, 1):
        after.append((1, 1, k))
    return [Z_ORDER[way].index(piece) for piece in after]


def kernel(
    a_ref, b_ref, w_ref, out_ref, av, wv, am, ab, bb, cb, qb, qs, rb, rs, sb, ob,
    l_s, a_s, a_r, y_s, y_r, z_s, z_r, k_s, k_r, x_s, x_r, o_s, o_r,
):
    pair, split = lax.axis_index("pair"), lax.axis_index("split")
    zh, y, core = pair // 16, (pair // 2) % 8, pair % 2
    x, zl = split // 4, split % 4
    z = zh * 4 + zl
    exchange = (zl, zl + 1 - 2 * (zl % 2), (zl + 2) % 4, 3 - zl)

    def device(x=x, y=y, z=z, core=core):
        return (z // 4 * 16 + y * 2 + core, x * 4 + z % 4)

    def remote(src, dst, send, recv, to):
        return pltpu.make_async_remote_copy(
            src_ref=src, dst_ref=dst, send_sem=send, recv_sem=recv, device_id=to, device_id_type=MESH
        )

    def up(v, by, n):
        return (v + by + n) % n

    partners = [device(z=zh * 4 + exchange[j]) for j in (1, 2, 3)]
    partners += [device(y=up(y, d, 8)) for d in range(1, 8)]
    partners += [device(x=up(x, d, 4)) for d in (1, 2, 3)]
    partners += [device(core=1 - core), device(z=up(z, 1, 8)), device(z=up(z, -1, 8))]
    barrier = pltpu.get_barrier_semaphore()
    for partner in partners:
        pl.semaphore_signal(barrier, inc=1, device_id=partner, device_id_type=MESH)

    def k_lanes(z_lo):
        return pl.ds(pl.multiple_of(z_lo * QS, 128), QS)

    def k_rows(z, k=None):
        if k is None:
            return pl.ds(pl.multiple_of(z * QS, 64), QS)
        return pl.ds(pl.multiple_of(z * QS + k * KS, 32), KS)

    my_lanes = pl.ds(pl.multiple_of(core * 128, 128), 128)

    loads = [
        pltpu.make_async_copy(w_ref, wv, l_s.at[0]),
        pltpu.make_async_copy(a_ref, av, l_s.at[1]),
    ] + [
        pltpu.make_async_copy(b_ref.at[:, pl.ds(h * 128, 128)], bb.at[h, k_rows(z), my_lanes], l_s.at[2 + h])
        for h in (0, 1)
    ]
    for load in loads:
        load.start()
    cb[1] = jnp.zeros(cb.shape[1:], F32)
    pl.semaphore_wait(barrier, len(partners))

    sent = []

    def start(copy):
        copy.start()
        sent.append(copy)

    def drain(n):
        for _ in range(n):
            sent.pop(0).wait_send()

    def a_copy(j):
        return remote(
            am.at[exchange[j]], ab.at[0, :, k_lanes(zl)], a_s.at[j - 1], a_r.at[j - 1],
            device(z=zh * 4 + exchange[j]),
        )

    def y_copy(way, i):
        d, j = Y_ORDER[way][i]
        sign = (-1, 1)[way]
        lanes = k_lanes(exchange[j])
        return remote(
            ab.at[PLACE[sign * (d - 1)], :, lanes], ab.at[PLACE[sign * d], :, lanes],
            y_s.at[way, i], y_r.at[way, i], device(y=up(y, -sign, 8)),
        )

    def z_copy(way, i):
        h, d, k = Z_ORDER[way][i]
        sign = (-1, 1)[way]
        piece = bb.at[h, k_rows(up(z, sign * (d - 1), 8), k), my_lanes]
        own = b_ref.at[pl.ds(k * KS, KS), pl.ds(h * 128, 128)]
        return remote(own if d == 1 else piece, piece, z_s.at[way, i], z_r.at[way, i], device(z=up(z, -sign, 8)))

    def k_copy(h, away, k):
        rows = pl.ds(pl.multiple_of(up(z, away, 8) * QS + k * 2 * KS, 64), 2 * KS)
        piece = bb.at[h, rows, my_lanes]
        at = (away + 8) % 8 * 2 + k
        own = b_ref.at[pl.ds(k * 2 * KS, 2 * KS), pl.ds(h * 128, 128)]
        return remote(piece if away else own, piece, k_s.at[h, at], k_r.at[h, at], device(core=1 - core))

    def x_copies(h, batch, d):
        lo, hi = BATCHES[h][batch]
        at = 2 * h + batch
        return (
            remote(
                qb.at[h, d - 1, lo:hi], rb.at[h, d - 1, lo:hi], x_s.at[at, d - 1, 0], x_r.at[at, d - 1, 0],
                device(x=up(x, d, 4)),
            ),
            remote(
                qs.at[at, d - 1], rs.at[at, d - 1], x_s.at[at, d - 1, 1], x_r.at[at, d - 1, 1],
                device(x=up(x, d, 4)),
            ),
        )

    def send_sums(h, batch):
        lo, hi = BATCHES[h][batch]
        at = 2 * h + batch
        for d in (2, 1, 3):
            part = cb[h, up(x, d, 4), lo:hi]
            top = jnp.maximum(jnp.max(jnp.abs(part), axis=1, keepdims=True), 1e-30)
            qb[h, d - 1, lo:hi] = jnp.round(part * (MOST / top)).astype(jnp.int32).astype(jnp.int16)
            step = (top * (1.0 / MOST)).reshape(4, 512)
            qs[at, d - 1, 0:4, :] = step[:, :256]
            qs[at, d - 1, 4:8, :] = step[:, 256:]
            for copy in x_copies(h, batch, d):
                start(copy)

    def o_copy(h, place):
        return remote(
            sb.at[h, place], ob.at[h, PLACE[-DELTA[place]]], o_s.at[h, place - 1],
            o_r.at[h, PLACE[-DELTA[place]] - 1], device(y=up(y, DELTA[place], 8)),
        )

    def product(h, lo, hi):
        rows = ab[lo:hi].reshape((hi - lo) * 64, 4 * QS)
        for half in (0, 1):
            part = jnp.dot(
                rows, bb[h, half * 4 * QS : (half + 1) * 4 * QS, :], preferred_element_type=F32
            ).reshape(hi - lo, 4, 16, 256)
            for xx in range(4):
                cb[h, xx, lo:hi, :, half * 256 : half * 256 + 256] = part[:, xx]

    def total(h, batch):
        lo, hi = BATCHES[h][batch]
        at = 2 * h + batch
        mine = cb[h, x, lo:hi]
        for d in (1, 2, 3):
            for copy in x_copies(h, batch, d):
                copy.wait_recv()
            step = jnp.concatenate([rs[at, d - 1, 0:4, :], rs[at, d - 1, 4:8, :]], axis=1).reshape(4, 1, 512)
            mine += rb[h, d - 1, lo:hi].astype(jnp.int32).astype(F32) * step
        sb[h, lo:hi] = mine.astype(BF16)
        for place in range(max(lo, 1), hi):
            start(o_copy(h, place))

    def place_result(h, place, piece):
        col = up(y, DELTA[place], 8) * 512 + h * 128
        for half in (0, 1):
            for cc in (0, 1):
                to = pl.multiple_of(half * 4096 + col + cc * 256, 128)
                from_ = half * 256 + cc * 128
                out_ref[:, pl.ds(to, 128)] = piece[:, from_ : from_ + 128]

    for kind, what in FIRST:
        if kind == "z":
            for k in what:
                for way in (0, 1):
                    start(z_copy(way, Z_ORDER[way].index((0, 1, k))))
            continue
        if what == 1:
            for load in loads[:2]:
                load.wait()
            keep = wv[...].astype(F32).astype(BF16).reshape(1, QS)
            for zz in range(4):
                for xx in range(4):
                    at = (xx * 4 + zz) * 16
                    am[zz, xx * 16 : xx * 16 + 16, :] = av[at : at + 16, :] * keep
            ab[0, :, k_lanes(zl)] = am[zl]
        start(a_copy(what))
        if what == 1:
            for way in (0, 1):
                start(y_copy(way, 0))
    for h in (0, 1):
        for k in (0, 1):
            start(k_copy(h, 0, k))
    for load in loads[2:]:
        load.wait()

    done = set()

    def step(kind, what):
        if kind == "a":
            a_copy(what).wait_recv()
            for way in (0, 1):
                start(y_copy(way, what))
        elif kind == "y":
            way, i = what
            y_copy(way, i).wait_recv()
            for after in follow_y(way, i):
                start(y_copy(way, after))
        else:
            way, i = what
            z_copy(way, i).wait_recv()
            for after in follow_z(way, i):
                start(z_copy(way, after))
            h, d, k = Z_ORDER[way][i]
            if k % 2:
                start(k_copy(h, (-1, 1)[way] * d, k // 2))
        done.add((kind, what))

    def wait_core(h, at):
        for k in (0, 1):
            k_copy(h, at, k).wait_recv()

    def add_product(at):
        owner = up(z, at, 8)
        lanes = pl.ds(pl.multiple_of(owner // 4 * 256, 128), 256)
        part = jnp.dot(
            ab[:, :, k_lanes(owner % 4)].reshape(512, QS), bb[1, k_rows(owner), :], preferred_element_type=F32
        ).reshape(8, 4, 16, 256)
        for xx in range(4):
            cb[1, xx, :, :, lanes] += part[:, xx]

    def ready(far):
        return all(("y", (way, i)) in done for way in (0, 1) for i in range(14) if Y_ORDER[way][i][0] <= far)

    h0_done = False
    sums = []
    behind = list(NEAR_FIRST)
    for kind, what in schedule():
        step(kind, what)
        if not h0_done and all(("z", (way, i)) in done for way in (0, 1) for i in range(28) if Z_ORDER[way][i][0] == 0):
            for at in range(8):
                wait_core(0, at)
            h0_done = True
        if h0_done:
            for batch, (lo, hi) in enumerate(BATCHES[0]):
                far = {4: 2, 8: 4}[hi]
                if ready(far) and batch not in sums:
                    sums.append(batch)
                    product(0, lo, hi)
                    send_sums(0, batch)
        if len(sums) == 2:
            arrived = {Z_ORDER[way][i][1] for way in (0, 1) for i in range(28) if ("z", (way, i)) in done and i + 2 < 28 and ("z", (way, i + 2)) in done and Z_ORDER[way][i][0] == 1 and Z_ORDER[way][i][2] == 3}
            if behind and (behind[0] == 0 or min(behind[0], 8 - behind[0]) in arrived):
                at = behind.pop(0)
                wait_core(1, at)
                add_product(at)
    for at in behind:
        wait_core(1, at)
        add_product(at)
    gathered = len(sent)
    for batch in (0, 1):
        send_sums(1, batch)
    for batch in (0, 1):
        total(0, batch)
    drain(gathered)
    place_result(0, 0, sb.at[0, 0])
    for place in range(1, 8):
        o_copy(0, PLACE[-DELTA[place]]).wait_recv()
        place_result(0, place, ob.at[0, place])
    total(1, 0)
    total(1, 1)
    place_result(1, 0, sb.at[1, 0])
    for place in range(1, 8):
        o_copy(1, PLACE[-DELTA[place]]).wait_recv()
        place_result(1, place, ob.at[1, place])
    drain(len(sent))


def on_device(integrals, normal_ops, window):
    dma = pltpu.SemaphoreType.DMA
    vmem = pl.BlockSpec(memory_space=pltpu.VMEM)
    return pl.pallas_call(
        kernel,
        out_shape=jax.ShapeDtypeStruct((16, 8192), BF16),
        in_specs=[pl.BlockSpec(memory_space=pl.ANY)] * 3,
        out_specs=vmem,
        scratch_shapes=[
            pltpu.VMEM((256, QS), BF16),
            pltpu.VMEM((QS,), jnp.int32),
            pltpu.VMEM((4, 64, QS), BF16),
            pltpu.VMEM((8, 64, 4 * QS), BF16),
            pltpu.VMEM((2, 8 * QS, 256), BF16),
            pltpu.VMEM((2, 4, 8, 16, 512), F32),
            pltpu.VMEM((2, 3, 8, 16, 512), jnp.int16),
            pltpu.VMEM((4, 3, 8, 256), F32),
            pltpu.VMEM((2, 3, 8, 16, 512), jnp.int16),
            pltpu.VMEM((4, 3, 8, 256), F32),
            pltpu.VMEM((2, 8, 16, 512), BF16),
            pltpu.VMEM((2, 8, 16, 512), BF16),
            dma((4,)),
            dma((3,)), dma((3,)),
            dma((2, 14)), dma((2, 14)),
            dma((2, 28)), dma((2, 28)),
            dma((2, 16)), dma((2, 16)),
            dma((4, 3, 2)), dma((4, 3, 2)),
            dma((2, 7)), dma((2, 7)),
        ],
        compiler_params=pltpu.CompilerParams(
            collective_id=0, has_side_effects=True, vmem_limit_bytes=54848 << 10
        ),
        cost_estimate=pl.CostEstimate(flops=2 * 512 * 1024 * 2560, bytes_accessed=1 << 20, transcendentals=0),
    )(integrals, normal_ops, window)


def solution(mesh):
    placed = (P("pair", "split"), P("split", "pair"), P("split"))
    return jax.shard_map(
        on_device, mesh=mesh, in_specs=placed, out_specs=P(("pair", "split"), None), check_vma=False
    )
```

```python
import jax
import jax.numpy as jnp
from jax import lax
from jax.experimental import pallas as pl
from jax.experimental.pallas import tpu as pltpu
from jax.sharding import PartitionSpec as P

MESH = pl.DeviceIdType.MESH
QS = 640
BF16, F32 = jnp.bfloat16, jnp.float32


DELTA = (0, 1, -1, 2, -2, 3, -3, 4)
PLACE = {delta: at for at, delta in enumerate(DELTA)} | {-4: 7}
Z_ORDER = tuple(
    tuple((h, d, k) for h in (0, 1) for d in (1, 2, 3, 4) for k in range(2) if d < 4 or k == way) for way in (0, 1)
)
KS = QS // 2
Y_ORDER = tuple(
    tuple((d, j) for d in (1, 2, 3) for j in range(4)) + tuple((4, j) for j in last)
    for last in ((0, 1), (2, 3))
)
MOST = 32600.0
NEAR_FIRST = (0, 1, 7, 2, 6, 3, 5, 4)
FIRST = (("a", 1), ("z", (0,)), ("a", 2), ("z", (1,)), ("a", 3))


def schedule(latency=3.2, piece=1.64, core=3.0):
    free, coming, order = {}, [], []

    def send(axis, way, what, load=1.0):
        end = max(send.now, free.get((axis, way), 0.0)) + load * piece
        free[axis, way] = end
        coming.append((end + latency, len(order) + len(coming), axis, way, what))

    send.now = 0.0
    for way in (0, 1):
        send("y", way, 0)
        for kind, what in FIRST:
            if kind == "a":
                send("z", way, ("a", what), 1.0 if what == 1 else 1.5)
            else:
                for k in what:
                    send("z", way, Z_ORDER[way].index((0, 1, k)))
    while coming:
        coming.sort()
        send.now, _, axis, way, what = coming.pop(0)
        if isinstance(what, tuple):
            if way == 0:
                order.append((send.now, *what))
                for to in (0, 1):
                    send("y", to, what[1])
            continue
        order.append((send.now, axis, (way, what)))
        for after in follow_y(way, what) if axis == "y" else follow_z(way, what):
            send(axis, way, after)
    rows = {far: max(t for t, axis, (way, i) in heard(order, "y") if Y_ORDER[way][i][0] <= far) for far in (2, 4)}
    columns = {(h, at): 0.0 for h in (0, 1) for at in range(8)}
    for t, _, (way, i) in heard(order, "z"):
        h, d, _ = Z_ORDER[way][i]
        at = (-d if way == 0 else d) % 8
        columns[h, at] = max(t, columns[h, at]) + 0.0
    first = max(t for (h, _), t in columns.items() if h == 0) + core
    order.append((max(rows[2], first), "p", 0))
    order.append((max(rows[4], first), "p", 1))
    after = max(rows[4], first)
    for at in NEAR_FIRST:
        after = max(after + 0.3, columns[1, at] + core)
        order.append((after, "q", at))
    order.sort(key=lambda event: event[0])
    return [event[1:] for event in order]


def heard(order, axis):
    return [event for event in order if event[1] == axis]


def follow_y(way, i):
    d, j = Y_ORDER[way][i]
    return [Y_ORDER[way].index((d + 1, j))] if (d + 1, j) in Y_ORDER[way] else []


def follow_z(way, i):
    h, d, k = Z_ORDER[way][i]
    after = [(h, d + 1, k)] if (h, d + 1, k) in Z_ORDER[way] else []
    if (h, d) == (0, 2):
        after.append((1, 1, k))
    return [Z_ORDER[way].index(piece) for piece in after]


def kernel(
    a_ref, b_ref, w_ref, out_ref, w0, w1, w2, w3, wf, ab, bb, cb, qb, qs, rb, rs, sb, ob,
    l_s, w_s, w_r, a_s, a_r, y_s, y_r, z_s, z_r, k_s, k_r, x_s, x_r, o_s, o_r,
):
    pair, split = lax.axis_index("pair"), lax.axis_index("split")
    zh, y, core = pair // 16, (pair // 2) % 8, pair % 2
    x, zl = split // 4, split % 4
    z = zh * 4 + zl
    exchange = (zl, zl + 1 - 2 * (zl % 2), (zl + 2) % 4, 3 - zl)

    def device(x=x, y=y, z=z, core=core):
        return (z // 4 * 16 + y * 2 + core, x * 4 + z % 4)

    def remote(src, dst, send, recv, to):
        return pltpu.make_async_remote_copy(
            src_ref=src, dst_ref=dst, send_sem=send, recv_sem=recv, device_id=to, device_id_type=MESH
        )

    def up(v, by, n):
        return (v + by + n) % n

    partners = [device(z=zh * 4 + exchange[j]) for j in (1, 2, 3)]
    partners += [device(y=up(y, d, 8)) for d in range(1, 8)]
    partners += [device(x=up(x, d, 4)) for d in (1, 2, 3)]
    partners += [device(core=1 - core), device(z=up(z, 1, 8)), device(z=up(z, -1, 8))]
    barrier = pltpu.get_barrier_semaphore()
    for partner in partners:
        pl.semaphore_signal(barrier, inc=1, device_id=partner, device_id_type=MESH)

    def k_lanes(z_lo):
        return pl.ds(pl.multiple_of(z_lo * QS, 128), QS)

    def k_rows(z, k=None):
        if k is None:
            return pl.ds(pl.multiple_of(z * QS, 64), QS)
        return pl.ds(pl.multiple_of(z * QS + k * KS, 32), KS)

    my_lanes = pl.ds(pl.multiple_of(core * 128, 128), 128)

    ws = (w0, w1, w2, w3)
    loads = [
        pltpu.make_async_copy(w_ref, w0, l_s.at[0]),
        pltpu.make_async_copy(a_ref.at[:, zl], ab.at[0, :, :, k_lanes(zl)], l_s.at[1]),
    ] + [
        pltpu.make_async_copy(b_ref.at[:, pl.ds(h * 128, 128)], bb.at[h, k_rows(z), my_lanes], l_s.at[2 + h])
        for h in (0, 1)
    ]
    for load in loads:
        load.start()
    cb[1] = jnp.zeros(cb.shape[1:], F32)
    pl.semaphore_wait(barrier, len(partners))

    sent = []

    def start(copy):
        copy.start()
        sent.append(copy)

    def drain(n):
        for _ in range(n):
            sent.pop(0).wait_send()

    def a_copy(j):
        return remote(
            a_ref.at[:, exchange[j]], ab.at[0, :, :, k_lanes(zl)], a_s.at[j - 1], a_r.at[j - 1],
            device(z=zh * 4 + exchange[j]),
        )

    def w_copy(j):
        return remote(w_ref, ws[j], w_s.at[j - 1], w_r.at[j - 1], device(z=zh * 4 + exchange[j]))

    def y_copy(way, i):
        d, j = Y_ORDER[way][i]
        sign = (-1, 1)[way]
        lanes = k_lanes(exchange[j])
        own = a_ref.at[:, zl]
        return remote(
            own if i == 0 else ab.at[PLACE[sign * (d - 1)], :, :, lanes], ab.at[PLACE[sign * d], :, :, lanes],
            y_s.at[way, i], y_r.at[way, i], device(y=up(y, -sign, 8)),
        )

    def z_copy(way, i):
        h, d, k = Z_ORDER[way][i]
        sign = (-1, 1)[way]
        piece = bb.at[h, k_rows(up(z, sign * (d - 1), 8), k), my_lanes]
        own = b_ref.at[pl.ds(k * KS, KS), pl.ds(h * 128, 128)]
        return remote(own if d == 1 else piece, piece, z_s.at[way, i], z_r.at[way, i], device(z=up(z, -sign, 8)))

    def k_copy(h, away, k):
        rows = pl.ds(pl.multiple_of(up(z, away, 8) * QS + k * KS, 64), KS)
        piece = bb.at[h, rows, my_lanes]
        at = (away + 8) % 8 * 2 + k
        own = b_ref.at[pl.ds(k * KS, KS), pl.ds(h * 128, 128)]
        return remote(piece if away else own, piece, k_s.at[h, at], k_r.at[h, at], device(core=1 - core))

    def x_copies(batch, d):
        to = device(x=up(x, d, 4))
        return tuple(
            remote(src.at[batch, d - 1], dst.at[batch, d - 1], x_s.at[batch, d - 1, at], x_r.at[batch, d - 1, at], to)
            for at, (src, dst) in enumerate(((qb, rb), (qs, rs)))
        )

    def units(batch):
        if batch < 2:
            lo, hi = batch * 4, batch * 4 + 4
            return ((0, 4, 0, 0, lo, hi), (4, 8, 0, 1, lo, hi))
        return ((0, 8, 1, (zh, 1 - zh)[batch - 2], 0, 8),)

    def send_sums(batch):
        for d in (2, 1, 3):
            steps = []
            for at, end, h, half, lo, hi in units(batch):
                part = cb[h, half, up(x, d, 4), lo:hi]
                top = jnp.maximum(jnp.max(jnp.abs(part), axis=1, keepdims=True), 1e-30)
                step = (top * (1.0 / MOST)).astype(BF16).astype(F32)
                qb[batch, d - 1, at:end] = jnp.round(part / step).astype(jnp.int32).astype(jnp.int16)
                steps.append(step.reshape(end - at, 256))
            steps = jnp.concatenate(steps, axis=0)
            qs[batch, d - 1] = jnp.concatenate([steps[:, :128], steps[:, 128:]], axis=0).astype(BF16)
            for copy in x_copies(batch, d):
                start(copy)

    def o_copy(batch, place):
        there = PLACE[-DELTA[place]]
        if batch < 2:
            src, dst = sb.at[0, place], ob.at[0, there]
        else:
            half = (zh, 1 - zh)[batch - 2]
            src, dst = sb.at[1, place, half], ob.at[1, there, half]
        at = max(batch - 1, 0)
        return remote(
            src, dst, o_s.at[at, place - 1], o_r.at[at, there - 1], device(y=up(y, DELTA[place], 8))
        )

    def total(batch):
        for d in (1, 2, 3):
            for copy in x_copies(batch, d):
                copy.wait_recv()
        for at, end, h, half, lo, hi in units(batch):
            mine = cb[h, half, x, lo:hi]
            for d in (1, 2, 3):
                steps = rs[batch, d - 1].astype(F32)
                step = jnp.concatenate([steps[at:end], steps[8 + at : 8 + end]], axis=1).reshape(end - at, 1, 256)
                mine += rb[batch, d - 1, at:end].astype(jnp.int32).astype(F32) * step
            sb[h, lo:hi, half] = mine.astype(BF16)
        for place in range(max(lo, 1), hi):
            start(o_copy(batch, place))

    def rows_of(block, w):
        return (block * w.reshape(1, 1, 1, w.shape[-1])).reshape(-1, w.shape[-1])

    def arrive_local():
        for load in loads:
            load.wait()
        for j in (1, 2, 3):
            w_copy(j).wait_recv()
        for j in range(4):
            wf[exchange[j]] = ws[j][...].astype(F32).astype(BF16).reshape(1, QS)

    def product(lo, hi):
        rows = rows_of(ab[lo:hi], jnp.concatenate([wf[at] for at in range(4)], axis=1))
        for half in (0, 1):
            part = jnp.dot(
                rows, bb[0, half * 4 * QS : (half + 1) * 4 * QS, :], preferred_element_type=F32
            ).reshape(hi - lo, 4, 16, 256)
            for xx in range(4):
                cb[0, half, xx, lo:hi] = part[:, xx]

    def add_product(at):
        owner = up(z, at, 8)
        part = jnp.dot(
            rows_of(ab[:, :, :, k_lanes(owner % 4)], wf[owner % 4]), bb[1, k_rows(owner), :],
            preferred_element_type=F32,
        ).reshape(8, 4, 16, 256)
        for xx in range(4):
            cb[1, owner // 4, xx] += part[:, xx]

    def wait_core(h, at):
        for k in (0, 1):
            k_copy(h, at, k).wait_recv()

    def place_result(h, place, half, piece):
        for cc in (0, 1):
            to = pl.multiple_of(half * 4096 + up(y, DELTA[place], 8) * 512 + cc * 256 + h * 128, 128)
            out_ref[:, pl.ds(to, 128)] = piece[:, cc * 128 : cc * 128 + 128]

    def place_all(batch):
        h = min(batch - 1, 1)
        for half in (0, 1) if h == 0 else ((zh, 1 - zh)[batch - 2],):
            place_result(h, 0, half, sb[h, 0, half])
        for place in range(1, 8):
            o_copy(batch, PLACE[-DELTA[place]]).wait_recv()
            for half in (0, 1) if h == 0 else ((zh, 1 - zh)[batch - 2],):
                place_result(h, place, half, ob[h, place, half])

    for kind, what in FIRST:
        if kind == "z":
            for k in what:
                for way in (0, 1):
                    start(z_copy(way, Z_ORDER[way].index((0, 1, k))))
            continue
        start(a_copy(what))
        if what == 1:
            for way in (0, 1):
                start(y_copy(way, 0))
    for h in (0, 1):
        for k in (0, 1):
            start(k_copy(h, 0, k))
    for j in (1, 2, 3):
        start(w_copy(j))

    def step(kind, what):
        if kind == "a":
            a_copy(what).wait_recv()
            for way in (0, 1):
                start(y_copy(way, what))
        elif kind == "y":
            way, i = what
            y_copy(way, i).wait_recv()
            for after in follow_y(way, i):
                start(y_copy(way, after))
        else:
            way, i = what
            z_copy(way, i).wait_recv()
            for after in follow_z(way, i):
                start(z_copy(way, after))
            h, d, k = Z_ORDER[way][i]
            start(k_copy(h, (-1, 1)[way] * d, k))

    for count, (kind, what) in enumerate(schedule()):
        if kind in "ayz":
            step(kind, what)
            if count > 30:
                drain(2)
        elif kind == "p":
            if what == 0:
                arrive_local()
                for at in range(8):
                    wait_core(0, at)
            product(what * 4, what * 4 + 4)
            send_sums(what)
        else:
            if what == 4:
                send_sums(2)
                total(0)
            wait_core(1, what)
            add_product(what)
    gathered = len(sent)
    send_sums(3)
    total(1)
    total(2)
    drain(gathered)
    place_all(1)
    total(3)
    drain(len(sent) - 7)
    place_all(2)
    place_all(3)
    drain(len(sent))


def on_device(integrals, normal_ops, window):
    dma = pltpu.SemaphoreType.DMA
    vmem = pl.BlockSpec(memory_space=pltpu.VMEM)
    return pl.pallas_call(
        kernel,
        out_shape=jax.ShapeDtypeStruct((16, 8192), BF16),
        in_specs=[pl.BlockSpec(memory_space=pl.ANY)] * 3,
        out_specs=vmem,
        scratch_shapes=[
            pltpu.VMEM((QS,), jnp.int32),
            pltpu.VMEM((QS,), jnp.int32),
            pltpu.VMEM((QS,), jnp.int32),
            pltpu.VMEM((QS,), jnp.int32),
            pltpu.VMEM((4, 1, QS), BF16),
            pltpu.VMEM((8, 4, 16, 4 * QS), BF16),
            pltpu.VMEM((2, 8 * QS, 256), BF16),
            pltpu.VMEM((2, 2, 4, 8, 16, 256), F32),
            pltpu.VMEM((4, 3, 8, 16, 256), jnp.int16),
            pltpu.VMEM((4, 3, 16, 128), BF16),
            pltpu.VMEM((4, 3, 8, 16, 256), jnp.int16),
            pltpu.VMEM((4, 3, 16, 128), BF16),
            pltpu.VMEM((2, 8, 2, 16, 256), BF16),
            pltpu.VMEM((2, 8, 2, 16, 256), BF16),
            dma((4,)),
            dma((3,)), dma((3,)),
            dma((3,)), dma((3,)),
            dma((2, 14)), dma((2, 14)),
            dma((2, 14)), dma((2, 14)),
            dma((2, 16)), dma((2, 16)),
            dma((4, 3, 2)), dma((4, 3, 2)),
            dma((3, 7)), dma((3, 7)),
        ],
        compiler_params=pltpu.CompilerParams(
            collective_id=0, has_side_effects=True, vmem_limit_bytes=54848 << 10
        ),
        cost_estimate=pl.CostEstimate(flops=2 * 512 * 1024 * 2560, bytes_accessed=1 << 20, transcendentals=0),
    )(integrals.reshape(4, 4, 16, QS), normal_ops, window)


def solution(mesh):
    placed = (P("pair", "split"), P("split", "pair"), P("split"))
    return jax.shard_map(
        on_device, mesh=mesh, in_specs=placed, out_specs=P(("pair", "split"), None), check_vma=False
    )
```

```python
import jax
import jax.numpy as jnp
from jax import lax
from jax.experimental import pallas as pl
from jax.experimental.pallas import tpu as pltpu
from jax.sharding import PartitionSpec as P

MESH = pl.DeviceIdType.MESH
QS = 640
BF16, F32 = jnp.bfloat16, jnp.float32


DELTA = (0, 1, -1, 2, -2, 3, -3, 4)
PLACE = {delta: at for at, delta in enumerate(DELTA)} | {-4: 7}
Z_ORDER = tuple(
    tuple((h, d, k) for h in (0, 1) for d in (1, 2, 3, 4) for k in range(2) if d < 4 or k == way) for way in (0, 1)
)
KS = QS // 2
Y_ORDER = tuple(
    tuple((d, j) for d in (1, 2, 3) for j in range(4)) + tuple((4, j) for j in last)
    for last in ((0, 1), (2, 3))
)
MOST = 32600.0
ORDER = (
    ("A", 2), ("A", 1), ("i", 0, 0), ("i", 0, 1), ("y", 1, 0), ("y", 0, 0), ("A", 3), ("z", 1, 0), ("a", 1),
    ("z", 0, 0), ("a", 2), ("i", 1, 0), ("y", 1, 1), ("z", 1, 1), ("z", 0, 1), ("y", 0, 1), ("y", 1, 4),
    ("a", 3), ("i", 1, 1), ("y", 1, 2), ("y", 0, 4), ("z", 0, 2), ("y", 0, 2), ("z", 1, 2), ("y", 1, 5),
    ("z", 0, 3), ("z", 1, 3), ("y", 0, 3), ("z", 0, 7), ("y", 0, 8), ("z", 1, 7), ("z", 1, 4), ("z", 1, 8),
    ("y", 0, 6), ("y", 1, 3), ("z", 1, 5), ("y", 1, 6), ("z", 0, 8), ("z", 1, 9), ("z", 0, 4), ("y", 1, 8),
    ("y", 0, 5), ("z", 0, 5), ("y", 1, 7), ("z", 0, 9), ("y", 0, 7), ("y", 0, 9), ("z", 1, 10), ("y", 1, 10),
    ("z", 1, 6), ("z", 0, 10), ("y", 0, 10), ("y", 1, 11), ("y", 1, 9), ("z", 0, 6), ("p", 0), ("y", 0, 12),
    ("z", 1, 12), ("z", 0, 11), ("z", 1, 11), ("y", 1, 12), ("y", 0, 13), ("z", 0, 12), ("y", 1, 13),
    ("y", 0, 11), ("q", 7), ("q", 6), ("p", 1), ("q", 0), ("q", 3), ("q", 2), ("q", 5), ("z", 1, 13),
    ("z", 0, 13), ("q", 1), ("q", 4),
)


def follow_y(way, i):
    d, j = Y_ORDER[way][i]
    return [Y_ORDER[way].index((d + 1, j))] if (d + 1, j) in Y_ORDER[way] else []


def follow_z(way, i):
    h, d, k = Z_ORDER[way][i]
    after = [(h, d + 1, k)] if (h, d + 1, k) in Z_ORDER[way] else []
    return [Z_ORDER[way].index(piece) for piece in after]


def kernel(
    a_ref, b_ref, w_ref, out_ref, w0, w1, w2, w3, wf, ab, bb, cb, qb, qs, rb, rs, sb, ob,
    l_s, w_s, w_r, a_s, a_r, y_s, y_r, z_s, z_r, k_s, k_r, x_s, x_r, o_s, o_r,
):
    pair, split = lax.axis_index("pair"), lax.axis_index("split")
    zh, y, core = pair // 16, (pair // 2) % 8, pair % 2
    x, zl = split // 4, split % 4
    z = zh * 4 + zl
    exchange = (zl, zl + 1 - 2 * (zl % 2), (zl + 2) % 4, 3 - zl)

    def device(x=x, y=y, z=z, core=core):
        return (z // 4 * 16 + y * 2 + core, x * 4 + z % 4)

    def remote(src, dst, send, recv, to):
        return pltpu.make_async_remote_copy(
            src_ref=src, dst_ref=dst, send_sem=send, recv_sem=recv, device_id=to, device_id_type=MESH
        )

    def up(v, by, n):
        return (v + by + n) % n

    partners = [device(z=zh * 4 + exchange[j]) for j in (1, 2, 3)]
    partners += [device(y=up(y, d, 8)) for d in range(1, 8)]
    partners += [device(x=up(x, d, 4)) for d in (1, 2, 3)]
    partners += [device(core=1 - core), device(z=up(z, 1, 8)), device(z=up(z, -1, 8))]
    barrier = pltpu.get_barrier_semaphore()
    for partner in partners:
        pl.semaphore_signal(barrier, inc=1, device_id=partner, device_id_type=MESH)

    def k_lanes(z_lo):
        return pl.ds(pl.multiple_of(z_lo * QS, 128), QS)

    def k_rows(z, k=None):
        if k is None:
            return pl.ds(pl.multiple_of(z * QS, 64), QS)
        return pl.ds(pl.multiple_of(z * QS + k * KS, 32), KS)

    my_lanes = pl.ds(pl.multiple_of(core * 128, 128), 128)

    ws = (w0, w1, w2, w3)
    loads = [
        pltpu.make_async_copy(w_ref, w0, l_s.at[0]),
        pltpu.make_async_copy(a_ref.at[:, zl], ab.at[0, :, :, k_lanes(zl)], l_s.at[1]),
    ] + [
        pltpu.make_async_copy(b_ref.at[:, pl.ds(h * 128, 128)], bb.at[h, k_rows(z), my_lanes], l_s.at[2 + h])
        for h in (0, 1)
    ]
    pl.semaphore_wait(barrier, len(partners))

    sent = []

    def start(copy):
        copy.start()
        sent.append(copy)

    def drain(n):
        for _ in range(n):
            sent.pop(0).wait_send()

    def a_copy(j):
        return remote(
            a_ref.at[:, exchange[j]], ab.at[0, :, :, k_lanes(zl)], a_s.at[j - 1], a_r.at[j - 1],
            device(z=zh * 4 + exchange[j]),
        )

    def w_copy(j):
        return remote(w_ref, ws[j], w_s.at[j - 1], w_r.at[j - 1], device(z=zh * 4 + exchange[j]))

    def y_copy(way, i):
        d, j = Y_ORDER[way][i]
        sign = (-1, 1)[way]
        lanes = k_lanes(exchange[j])
        own = a_ref.at[:, zl]
        return remote(
            own if i == 0 else ab.at[PLACE[sign * (d - 1)], :, :, lanes], ab.at[PLACE[sign * d], :, :, lanes],
            y_s.at[way, i], y_r.at[way, i], device(y=up(y, -sign, 8)),
        )

    def z_copy(way, i):
        h, d, k = Z_ORDER[way][i]
        sign = (-1, 1)[way]
        piece = bb.at[h, k_rows(up(z, sign * (d - 1), 8), k), my_lanes]
        own = b_ref.at[pl.ds(k * KS, KS), pl.ds(h * 128, 128)]
        return remote(own if d == 1 else piece, piece, z_s.at[way, i], z_r.at[way, i], device(z=up(z, -sign, 8)))

    def k_copy(h, away, k):
        rows = pl.ds(pl.multiple_of(up(z, away, 8) * QS + k * KS, 64), KS)
        piece = bb.at[h, rows, my_lanes]
        at = (away + 8) % 8 * 2 + k
        own = b_ref.at[pl.ds(k * KS, KS), pl.ds(h * 128, 128)]
        return remote(piece if away else own, piece, k_s.at[h, at], k_r.at[h, at], device(core=1 - core))

    def x_copies(batch, d):
        to = device(x=up(x, d, 4))
        n = units(batch)[-1][1]
        return tuple(
            remote(src, dst, x_s.at[batch, d - 1, at], x_r.at[batch, d - 1, at], to)
            for at, (src, dst) in enumerate((
                (qb.at[batch, d - 1, 0:n], rb.at[batch, d - 1, 0:n]), (qs.at[batch, d - 1], rs.at[batch, d - 1])
            ))
        )

    def units(batch):
        if batch < 2:
            lo, hi = batch * 4, batch * 4 + 4
            return ((0, 4, 0, 0, lo, hi), (4, 8, 0, 1, lo, hi))
        if batch == 2:
            return ((0, 8, 1, zh, 0, 8),)
        return ((0, 4, 1, 1 - zh, (4, 0)[batch - 3], (8, 4)[batch - 3]),)

    def send_sums(batch):
        for d in (2, 1, 3):
            steps = []
            for at, end, h, half, lo, hi in units(batch):
                part = cb[h, half, up(x, d, 4), lo:hi]
                top = jnp.maximum(jnp.max(jnp.abs(part), axis=1, keepdims=True), 1e-30)
                step = (top * (1.0 / MOST)).astype(BF16).astype(F32)
                qb[batch, d - 1, at:end] = jnp.round(part / step).astype(jnp.int32).astype(jnp.int16)
                steps.append(step.reshape(end - at, 256))
            if end == 4:
                steps.append(jnp.zeros((4, 256), F32))
            steps = jnp.concatenate(steps, axis=0)
            qs[batch, d - 1] = jnp.concatenate([steps[:, :128], steps[:, 128:]], axis=0).astype(BF16)
            for copy in x_copies(batch, d):
                start(copy)

    def o_copy(batch, place):
        there = PLACE[-DELTA[place]]
        if batch < 2:
            src, dst = sb.at[0, place], ob.at[0, there]
        else:
            half = (zh, 1 - zh, 1 - zh)[batch - 2]
            src, dst = sb.at[1, place, half], ob.at[1, there, half]
        at = min(max(batch - 1, 0), 2)
        return remote(
            src, dst, o_s.at[at, place - 1], o_r.at[at, there - 1], device(y=up(y, DELTA[place], 8))
        )

    def total(batch):
        for d in (1, 2, 3):
            for copy in x_copies(batch, d):
                copy.wait_recv()
        for at, end, h, half, lo, hi in units(batch):
            mine = cb[h, half, x, lo:hi]
            for d in (1, 2, 3):
                steps = rs[batch, d - 1].astype(F32)
                step = jnp.concatenate([steps[at:end], steps[8 + at : 8 + end]], axis=1).reshape(end - at, 1, 256)
                mine += rb[batch, d - 1, at:end].astype(jnp.int32).astype(F32) * step
            sb[h, lo:hi, half] = mine.astype(BF16)
        for place in range(max(lo, 1), hi):
            start(o_copy(batch, place))

    def rows_of(block, w):
        return (block * w.reshape(1, 1, 1, w.shape[-1])).reshape(-1, w.shape[-1])

    def arrive_local():
        cb[1] = jnp.zeros(cb.shape[1:], F32)
        for load in loads:
            load.wait()
        for j in (1, 2, 3):
            w_copy(j).wait_recv()
        for j in range(4):
            wf[exchange[j]] = ws[j][...].astype(F32).astype(BF16).reshape(1, QS)

    def product(lo, hi):
        rows = rows_of(ab[lo:hi], jnp.concatenate([wf[at] for at in range(4)], axis=1))
        for half in (0, 1):
            part = jnp.dot(
                rows, bb[0, half * 4 * QS : (half + 1) * 4 * QS, :], preferred_element_type=F32
            ).reshape(hi - lo, 4, 16, 256)
            for xx in range(4):
                cb[0, half, xx, lo:hi] = part[:, xx]

    def add_product(at):
        owner = up(z, at, 8)
        part = jnp.dot(
            rows_of(ab[:, :, :, k_lanes(owner % 4)], wf[owner % 4]), bb[1, k_rows(owner), :],
            preferred_element_type=F32,
        ).reshape(8, 4, 16, 256)
        for xx in range(4):
            cb[1, owner // 4, xx] += part[:, xx]

    def wait_core(h, at):
        for k in (0, 1):
            k_copy(h, at, k).wait_recv()

    def place_result(h, place, half, piece):
        for cc in (0, 1):
            to = pl.multiple_of(half * 4096 + up(y, DELTA[place], 8) * 512 + cc * 256 + h * 128, 128)
            out_ref[:, pl.ds(to, 128)] = piece[:, cc * 128 : cc * 128 + 128]

    def place_all(batch):
        h = min(batch - 1, 1)
        for half in (0, 1) if h == 0 else ((zh, 1 - zh)[batch - 2],):
            place_result(h, 0, half, sb[h, 0, half])
        for place in range(1, 8):
            o_copy(batch, PLACE[-DELTA[place]]).wait_recv()
            for half in (0, 1) if h == 0 else ((zh, 1 - zh)[batch - 2],):
                place_result(h, place, half, ob[h, place, half])

    def step(kind, what):
        if kind == "a":
            a_copy(what[0]).wait_recv()
            for way in (0, 1):
                start(y_copy(way, what[0]))
        elif kind == "y":
            way, i = what
            y_copy(way, i).wait_recv()
            for after in follow_y(way, i):
                start(y_copy(way, after))
        else:
            way, i = what
            z_copy(way, i).wait_recv()
            for after in follow_z(way, i):
                start(z_copy(way, after))
            h, d, k = Z_ORDER[way][i]
            start(k_copy(h, (-1, 1)[way] * d, k))

    for load in loads:
        load.start()
    for count, (kind, *what) in enumerate(ORDER):
        if kind == "A":
            start(a_copy(what[0]))
            if what[0] == 1:
                for way in (0, 1):
                    start(y_copy(way, 0))
        elif kind == "i":
            h, k = what
            for way in (0, 1):
                start(z_copy(way, Z_ORDER[way].index((h, 1, k))))
            start(k_copy(h, 0, k))
            if (h, k) == (0, 0):
                for j in (1, 2, 3):
                    start(w_copy(j))
        elif kind in "ayz":
            step(kind, what)
            if count > 40:
                drain(2)
        elif kind == "p":
            if what[0] == 0:
                arrive_local()
                for at in range(8):
                    wait_core(0, at)
            product(what[0] * 4, what[0] * 4 + 4)
            send_sums(what[0])
        else:
            if what[0] == 4:
                send_sums(2)
                total(0)
            wait_core(1, what[0])
            add_product(what[0])
    gathered = len(sent)
    send_sums(3)
    send_sums(4)
    total(1)
    total(2)
    drain(gathered)
    place_all(1)
    total(3)
    total(4)
    drain(len(sent) - 7)
    place_all(2)
    place_all(3)
    drain(len(sent))


def on_device(integrals, normal_ops, window):
    dma = pltpu.SemaphoreType.DMA
    vmem = pl.BlockSpec(memory_space=pltpu.VMEM)
    return pl.pallas_call(
        kernel,
        out_shape=jax.ShapeDtypeStruct((16, 8192), BF16),
        in_specs=[pl.BlockSpec(memory_space=pl.ANY)] * 3,
        out_specs=vmem,
        scratch_shapes=[
            pltpu.VMEM((QS,), jnp.int32),
            pltpu.VMEM((QS,), jnp.int32),
            pltpu.VMEM((QS,), jnp.int32),
            pltpu.VMEM((QS,), jnp.int32),
            pltpu.VMEM((4, 1, QS), BF16),
            pltpu.VMEM((8, 4, 16, 4 * QS), BF16),
            pltpu.VMEM((2, 8 * QS, 256), BF16),
            pltpu.VMEM((2, 2, 4, 8, 16, 256), F32),
            pltpu.VMEM((5, 3, 8, 16, 256), jnp.int16),
            pltpu.VMEM((5, 3, 16, 128), BF16),
            pltpu.VMEM((5, 3, 8, 16, 256), jnp.int16),
            pltpu.VMEM((5, 3, 16, 128), BF16),
            pltpu.VMEM((2, 8, 2, 16, 256), BF16),
            pltpu.VMEM((2, 8, 2, 16, 256), BF16),
            dma((4,)),
            dma((3,)), dma((3,)),
            dma((3,)), dma((3,)),
            dma((2, 14)), dma((2, 14)),
            dma((2, 14)), dma((2, 14)),
            dma((2, 16)), dma((2, 16)),
            dma((5, 3, 2)), dma((5, 3, 2)),
            dma((3, 7)), dma((3, 7)),
        ],
        compiler_params=pltpu.CompilerParams(
            collective_id=0, has_side_effects=True, vmem_limit_bytes=54848 << 10
        ),
        cost_estimate=pl.CostEstimate(flops=2 * 512 * 1024 * 2560, bytes_accessed=1 << 20, transcendentals=0),
    )(integrals.reshape(4, 4, 16, QS), normal_ops, pltpu.with_memory_space_constraint(window, pltpu.HBM))


def solution(mesh):
    placed = (P("pair", "split"), P("split", "pair"), P("split"))
    return jax.shard_map(
        on_device, mesh=mesh, in_specs=placed, out_specs=P(("pair", "split"), None), check_vma=False
    )
```

```python
import jax
import jax.numpy as jnp
from jax import lax
from jax.experimental import pallas as pl
from jax.experimental.pallas import tpu as pltpu
from jax.sharding import PartitionSpec as P

MESH = pl.DeviceIdType.MESH
QS = 640
BF16, F32 = jnp.bfloat16, jnp.float32


DELTA = (0, 1, -1, 2, -2, 3, -3, 4)
PLACE = {delta: at for at, delta in enumerate(DELTA)} | {-4: 7}
Z_ORDER = tuple(
    tuple((h, d, k) for h in (0, 1) for d in (1, 2, 3, 4) for k in range(2) if d < 4 or k == way) for way in (0, 1)
)
KS = QS // 2
Y_ORDER = tuple(
    tuple((d, j) for d in (1, 2, 3) for j in range(4)) + tuple((4, j) for j in last)
    for last in ((0, 1), (2, 3))
)
MOST = 32600.0
ORDER = (
    ("A", 3), ("A", 1), ("i", 0, 0), ("y", 1, 0), ("i", 0, 1), ("y", 0, 0), ("a", 3), ("A", 2), ("a", 1),
    ("z", 0, 0), ("z", 1, 1), ("i", 1, 1), ("y", 0, 4), ("i", 1, 0), ("y", 1, 4), ("z", 1, 0), ("z", 0, 1),
    ("a", 2), ("y", 0, 3), ("z", 0, 2), ("y", 1, 3), ("z", 0, 8), ("z", 1, 3), ("y", 0, 1), ("y", 1, 2),
    ("y", 1, 1), ("y", 0, 2), ("z", 0, 7), ("z", 1, 8), ("y", 1, 7), ("z", 1, 2), ("y", 1, 6), ("y", 0, 8),
    ("y", 0, 5), ("z", 0, 3), ("z", 1, 5), ("z", 1, 7), ("z", 0, 4), ("y", 1, 5), ("z", 0, 9), ("y", 0, 12),
    ("y", 0, 7), ("z", 0, 10), ("z", 1, 4), ("z", 0, 5), ("z", 1, 10), ("y", 1, 10), ("y", 0, 6), ("z", 1, 6),
    ("z", 1, 9), ("y", 1, 8), ("y", 1, 9), ("z", 0, 6), ("y", 1, 11), ("y", 0, 9), ("z", 0, 11), ("p", 0),
    ("y", 0, 11), ("y", 0, 10), ("z", 1, 11), ("y", 0, 13), ("y", 1, 13), ("z", 1, 12), ("y", 1, 12),
    ("z", 0, 12), ("p", 1), ("q", 2), ("q", 6), ("q", 0), ("q", 5), ("q", 3), ("q", 1), ("z", 0, 13), ("q", 7),
    ("z", 1, 13), ("q", 4),
)


def follow_y(way, i):
    d, j = Y_ORDER[way][i]
    return [Y_ORDER[way].index((d + 1, j))] if (d + 1, j) in Y_ORDER[way] else []


def follow_z(way, i):
    h, d, k = Z_ORDER[way][i]
    after = [(h, d + 1, k)] if (h, d + 1, k) in Z_ORDER[way] else []
    return [Z_ORDER[way].index(piece) for piece in after]


def kernel(
    a_ref, b_ref, w_ref, out_ref, w0, w1, w2, w3, wf, ab, bb, cb, qb, qs, rb, rs, sb, ob,
    l_s, w_s, w_r, a_s, a_r, y_s, y_r, z_s, z_r, k_s, k_r, x_s, x_r, o_s, o_r,
):
    pair, split = lax.axis_index("pair"), lax.axis_index("split")
    zh, y, core = pair // 16, (pair // 2) % 8, pair % 2
    x, zl = split // 4, split % 4
    z = zh * 4 + zl
    exchange = (zl, zl + 1 - 2 * (zl % 2), (zl + 2) % 4, 3 - zl)

    def device(x=x, y=y, z=z, core=core):
        return (z // 4 * 16 + y * 2 + core, x * 4 + z % 4)

    def remote(src, dst, send, recv, to):
        return pltpu.make_async_remote_copy(
            src_ref=src, dst_ref=dst, send_sem=send, recv_sem=recv, device_id=to, device_id_type=MESH
        )

    def up(v, by, n):
        return (v + by + n) % n

    partners = [device(z=zh * 4 + exchange[j]) for j in (1, 2, 3)]
    partners += [device(y=up(y, d, 8)) for d in range(1, 8)]
    partners += [device(x=up(x, d, 4)) for d in (1, 2, 3)]
    partners += [device(core=1 - core), device(z=up(z, 1, 8)), device(z=up(z, -1, 8))]
    barrier = pltpu.get_barrier_semaphore()
    for partner in partners:
        pl.semaphore_signal(barrier, inc=1, device_id=partner, device_id_type=MESH)

    def k_lanes(z_lo):
        return pl.ds(pl.multiple_of(z_lo * QS, 128), QS)

    def k_rows(z, k=None):
        if k is None:
            return pl.ds(pl.multiple_of(z * QS, 64), QS)
        return pl.ds(pl.multiple_of(z * QS + k * KS, 32), KS)

    my_lanes = pl.ds(pl.multiple_of(core * 128, 128), 128)

    ws = (w0, w1, w2, w3)
    loads = [
        pltpu.make_async_copy(w_ref, w0, l_s.at[0]),
        pltpu.make_async_copy(a_ref.at[:, zl], ab.at[0, :, :, k_lanes(zl)], l_s.at[1]),
    ] + [
        pltpu.make_async_copy(b_ref.at[:, pl.ds(h * 128, 128)], bb.at[h, k_rows(z), my_lanes], l_s.at[2 + h])
        for h in (0, 1)
    ]
    pl.semaphore_wait(barrier, len(partners))

    sent = []

    def start(copy):
        copy.start()
        sent.append(copy)

    def drain(n):
        for _ in range(n):
            sent.pop(0).wait_send()

    def a_copy(j):
        return remote(
            a_ref.at[:, exchange[j]], ab.at[0, :, :, k_lanes(zl)], a_s.at[j - 1], a_r.at[j - 1],
            device(z=zh * 4 + exchange[j]),
        )

    def w_copy(j):
        return remote(w_ref, ws[j], w_s.at[j - 1], w_r.at[j - 1], device(z=zh * 4 + exchange[j]))

    def y_copy(way, i):
        d, j = Y_ORDER[way][i]
        sign = (-1, 1)[way]
        lanes = k_lanes(exchange[j])
        own = a_ref.at[:, zl]
        return remote(
            own if i == 0 else ab.at[PLACE[sign * (d - 1)], :, :, lanes], ab.at[PLACE[sign * d], :, :, lanes],
            y_s.at[way, i], y_r.at[way, i], device(y=up(y, -sign, 8)),
        )

    def z_copy(way, i):
        h, d, k = Z_ORDER[way][i]
        sign = (-1, 1)[way]
        piece = bb.at[h, k_rows(up(z, sign * (d - 1), 8), k), my_lanes]
        own = b_ref.at[pl.ds(k * KS, KS), pl.ds(h * 128, 128)]
        return remote(own if d == 1 else piece, piece, z_s.at[way, i], z_r.at[way, i], device(z=up(z, -sign, 8)))

    def k_copy(h, away, k):
        rows = pl.ds(pl.multiple_of(up(z, away, 8) * QS + k * KS, 64), KS)
        piece = bb.at[h, rows, my_lanes]
        at = (away + 8) % 8 * 2 + k
        own = b_ref.at[pl.ds(k * KS, KS), pl.ds(h * 128, 128)]
        return remote(piece if away else own, piece, k_s.at[h, at], k_r.at[h, at], device(core=1 - core))

    def x_copies(batch, d):
        to = device(x=up(x, d, 4))
        n = units(batch)[-1][1]
        return tuple(
            remote(src, dst, x_s.at[batch, d - 1, at], x_r.at[batch, d - 1, at], to)
            for at, (src, dst) in enumerate((
                (qb.at[batch, d - 1, 0:n], rb.at[batch, d - 1, 0:n]), (qs.at[batch, d - 1], rs.at[batch, d - 1])
            ))
        )

    def units(batch):
        if batch < 2:
            lo, hi = batch * 4, batch * 4 + 4
            return ((0, 4, 0, 0, lo, hi), (4, 8, 0, 1, lo, hi))
        if batch == 2:
            return ((0, 8, 1, zh, 0, 8),)
        return ((0, 4, 1, 1 - zh, (4, 0)[batch - 3], (8, 4)[batch - 3]),)

    def send_sums(batch):
        for d in (2, 1, 3):
            steps = []
            for at, end, h, half, lo, hi in units(batch):
                part = cb[h, half, up(x, d, 4), lo:hi]
                top = jnp.maximum(jnp.max(jnp.abs(part), axis=1, keepdims=True), 1e-30)
                step = (top * (1.0 / MOST)).astype(BF16).astype(F32)
                qb[batch, d - 1, at:end] = jnp.round(part / step).astype(jnp.int32).astype(jnp.int16)
                steps.append(step.reshape(end - at, 256))
            if end == 4:
                steps.append(jnp.zeros((4, 256), F32))
            steps = jnp.concatenate(steps, axis=0)
            qs[batch, d - 1] = jnp.concatenate([steps[:, :128], steps[:, 128:]], axis=0).astype(BF16)
            for copy in x_copies(batch, d):
                start(copy)

    def o_copy(batch, place):
        there = PLACE[-DELTA[place]]
        if batch < 2:
            src, dst = sb.at[0, place], ob.at[0, there]
        else:
            half = (zh, 1 - zh, 1 - zh)[batch - 2]
            src, dst = sb.at[1, place, half], ob.at[1, there, half]
        at = min(max(batch - 1, 0), 2)
        return remote(
            src, dst, o_s.at[at, place - 1], o_r.at[at, there - 1], device(y=up(y, DELTA[place], 8))
        )

    def total(batch):
        for d in (1, 2, 3):
            for copy in x_copies(batch, d):
                copy.wait_recv()
        for at, end, h, half, lo, hi in units(batch):
            mine = cb[h, half, x, lo:hi]
            for d in (1, 2, 3):
                steps = rs[batch, d - 1].astype(F32)
                step = jnp.concatenate([steps[at:end], steps[8 + at : 8 + end]], axis=1).reshape(end - at, 1, 256)
                mine += rb[batch, d - 1, at:end].astype(jnp.int32).astype(F32) * step
            sb[h, lo:hi, half] = mine.astype(BF16)
        for place in range(max(lo, 1), hi):
            start(o_copy(batch, place))

    def rows_of(block, w):
        return (block * w.reshape(1, 1, 1, w.shape[-1])).reshape(-1, w.shape[-1])

    def arrive_local():
        cb[1] = jnp.zeros(cb.shape[1:], F32)
        for load in loads:
            load.wait()
        for j in (1, 2, 3):
            w_copy(j).wait_recv()
        for j in range(4):
            wf[exchange[j]] = ws[j][...].astype(F32).astype(BF16).reshape(1, QS)

    def product(lo, hi):
        rows = rows_of(ab[lo:hi], jnp.concatenate([wf[at] for at in range(4)], axis=1))
        for half in (0, 1):
            part = jnp.dot(
                rows, bb[0, half * 4 * QS : (half + 1) * 4 * QS, :], preferred_element_type=F32
            ).reshape(hi - lo, 4, 16, 256)
            for xx in range(4):
                cb[0, half, xx, lo:hi] = part[:, xx]

    def add_product(at):
        owner = up(z, at, 8)
        part = jnp.dot(
            rows_of(ab[:, :, :, k_lanes(owner % 4)], wf[owner % 4]), bb[1, k_rows(owner), :],
            preferred_element_type=F32,
        ).reshape(8, 4, 16, 256)
        for xx in range(4):
            cb[1, owner // 4, xx] += part[:, xx]

    def wait_core(h, at):
        for k in (0, 1):
            k_copy(h, at, k).wait_recv()

    def place_result(h, place, half, piece):
        for cc in (0, 1):
            to = pl.multiple_of(half * 4096 + up(y, DELTA[place], 8) * 512 + cc * 256 + h * 128, 128)
            out_ref[:, pl.ds(to, 128)] = piece[:, cc * 128 : cc * 128 + 128]

    def place_all(batch):
        h = min(batch - 1, 1)
        for half in (0, 1) if h == 0 else ((zh, 1 - zh)[batch - 2],):
            place_result(h, 0, half, sb[h, 0, half])
        for place in range(1, 8):
            o_copy(batch, PLACE[-DELTA[place]]).wait_recv()
            for half in (0, 1) if h == 0 else ((zh, 1 - zh)[batch - 2],):
                place_result(h, place, half, ob[h, place, half])

    def step(kind, what):
        if kind == "a":
            a_copy(what[0]).wait_recv()
            for way in (0, 1):
                start(y_copy(way, what[0]))
        elif kind == "y":
            way, i = what
            y_copy(way, i).wait_recv()
            for after in follow_y(way, i):
                start(y_copy(way, after))
        else:
            way, i = what
            z_copy(way, i).wait_recv()
            for after in follow_z(way, i):
                start(z_copy(way, after))
            h, d, k = Z_ORDER[way][i]
            start(k_copy(h, (-1, 1)[way] * d, k))

    for load in loads:
        load.start()
    for count, (kind, *what) in enumerate(ORDER):
        if kind == "A":
            start(a_copy(what[0]))
            if what[0] == 1:
                for way in (0, 1):
                    start(y_copy(way, 0))
        elif kind == "i":
            h, k = what
            for way in (0, 1):
                start(z_copy(way, Z_ORDER[way].index((h, 1, k))))
            start(k_copy(h, 0, k))
            if (h, k) == (0, 0):
                for j in (1, 2, 3):
                    start(w_copy(j))
        elif kind in "ayz":
            step(kind, what)
            if count > 40:
                drain(2)
        elif kind == "p":
            if what[0] == 0:
                arrive_local()
                for at in range(8):
                    wait_core(0, at)
            product(what[0] * 4, what[0] * 4 + 4)
            send_sums(what[0])
        else:
            if what[0] == 4:
                send_sums(2)
                total(0)
            wait_core(1, what[0])
            add_product(what[0])
    gathered = len(sent)
    send_sums(3)
    send_sums(4)
    total(1)
    total(2)
    drain(gathered)
    place_all(1)
    total(3)
    total(4)
    drain(len(sent) - 7)
    place_all(2)
    place_all(3)
    drain(len(sent))


def on_device(integrals, normal_ops, window):
    dma = pltpu.SemaphoreType.DMA
    vmem = pl.BlockSpec(memory_space=pltpu.VMEM)
    return pl.pallas_call(
        kernel,
        out_shape=jax.ShapeDtypeStruct((16, 8192), BF16),
        in_specs=[pl.BlockSpec(memory_space=pl.ANY)] * 3,
        out_specs=vmem,
        scratch_shapes=[
            pltpu.VMEM((QS,), jnp.int32),
            pltpu.VMEM((QS,), jnp.int32),
            pltpu.VMEM((QS,), jnp.int32),
            pltpu.VMEM((QS,), jnp.int32),
            pltpu.VMEM((4, 1, QS), BF16),
            pltpu.VMEM((8, 4, 16, 4 * QS), BF16),
            pltpu.VMEM((2, 8 * QS, 256), BF16),
            pltpu.VMEM((2, 2, 4, 8, 16, 256), F32),
            pltpu.VMEM((5, 3, 8, 16, 256), jnp.int16),
            pltpu.VMEM((5, 3, 16, 128), BF16),
            pltpu.VMEM((5, 3, 8, 16, 256), jnp.int16),
            pltpu.VMEM((5, 3, 16, 128), BF16),
            pltpu.VMEM((2, 8, 2, 16, 256), BF16),
            pltpu.VMEM((2, 8, 2, 16, 256), BF16),
            dma((4,)),
            dma((3,)), dma((3,)),
            dma((3,)), dma((3,)),
            dma((2, 14)), dma((2, 14)),
            dma((2, 14)), dma((2, 14)),
            dma((2, 16)), dma((2, 16)),
            dma((5, 3, 2)), dma((5, 3, 2)),
            dma((3, 7)), dma((3, 7)),
        ],
        compiler_params=pltpu.CompilerParams(
            collective_id=0, has_side_effects=True, vmem_limit_bytes=54848 << 10
        ),
        cost_estimate=pl.CostEstimate(flops=2 * 512 * 1024 * 2560, bytes_accessed=1 << 20, transcendentals=0),
    )(integrals.reshape(4, 4, 16, QS), normal_ops, pltpu.with_memory_space_constraint(window, pltpu.HBM))


def solution(mesh):
    placed = (P("pair", "split"), P("split", "pair"), P("split"))
    return jax.shard_map(
        on_device, mesh=mesh, in_specs=placed, out_specs=P(("pair", "split"), None), check_vma=False
    )
```
